256 devices in a mesh: ta: 4 (over z_hi), ha: 8 (over x, core), wa: 8 (over y, z_lo).
Axes of the slice: x: 4, y: 4, z: 8 (z_hi: 4, z_lo: 2; z = z_hi * 2 + z_lo), core: 2. Of those that a mesh axis runs over, the one named last changes fastest.
Arguments:
- clip: bfloat16 [8, 32, 128, 256], P('ta', 'ha', 'wa'), may hold values from -6 to 6
- conv_weight: bfloat16 [6912, 256], replicated, may hold values from -0.078125 to 0.078125
- down_weight: bfloat16 [6912, 256], replicated, may hold values from -0.078125 to 0.078125
- out_cotangent: bfloat16 [4, 16, 64, 256], P('ta', 'ha', 'wa'), may hold values from -6 to 6
Outputs:
- grad_clip: bfloat16 [8, 32, 128, 256], P('ta', 'ha', 'wa')
- grad_conv: float32 [6912, 256], P(('ha', 'wa'), 'ta')
- grad_down: float32 [6912, 256], P(('ha', 'wa'), 'ta')
The draws below stay inside these ranges and needn't reach their ends.
All inputs are finite; a program needn't handle non-finite values.
Results may differ from the reference program's by a relative error of at most 0.014.
Values may be sent and summed in bfloat16 or wider, within the bound.
No kernel may reach another device: no remote copies, remote signals or barrier semaphores. Data moves between devices by JAX's collectives and lax.ppermute only.
A program may use at most 64 MiB of HBM per device.

```python
import jax
import jax.numpy as jnp
from jax import lax

C = 256
NT = 8
NH = 32
NW = 128


def level_of(stream_key, shape, split, smallest, high):
    loudness = 1.0
    for position, blocks in split:
        draws = jax.random.uniform(jax.random.fold_in(jax.random.fold_in(stream_key, 6), position), (blocks,), jnp.float32, smallest / len(split), high / len(split))
        loudness = loudness * jnp.repeat(jnp.exp(draws), shape[position] // blocks).reshape((-1,) + (1,) * (len(shape) - 1 - position))
    return loudness


def bell_draw(own_key, dims, scale, most, pieces=(), dtype=jnp.bfloat16):
    drawn = scale * jax.random.normal(own_key, dims, jnp.float32)
    if pieces:
        drawn = drawn * level_of(own_key, dims, pieces, -0.22, 0.18)
    return jnp.clip(drawn, -most, most).astype(dtype)


def setup_inputs(seed: int = 0) -> dict:
    splits = jax.random.split(jax.random.key(seed), 5)
    return {
        "clip": bell_draw(splits[0], (NT, NH, NW, C), 1.0, 6.0, ((0, 4), (1, 8), (2, 8))),
        "conv_weight": bell_draw(splits[1], (27 * C, C), (27 * C) ** -0.5, 0.078125),
        "down_weight": bell_draw(splits[2], (27 * C, C), (27 * C) ** -0.5, 0.078125),
        "out_cotangent": bell_draw(splits[3], (NT // 2, NH // 2, NW // 2, C), 1.0, 6.0, ((0, 4), (1, 8), (2, 8))),
    }


def convolve(inputs, kernel, strides, padding):
    return lax.conv_general_dilated(inputs, kernel, strides, padding, dimension_numbers=('NDHWC', 'DHWIO', 'NDHWC'), precision=lax.Precision.HIGHEST)

def first_layer(inputs, kernel):
    return convolve(inputs, kernel, (1, 1, 1), [(2, 0), (1, 1), (1, 1)])

def down_layer(inputs, kernel):
    return convolve(inputs, kernel, (2, 2, 2), [(2, 0), (1, 0), (1, 0)])

def reference(clip, conv_weight, down_weight, out_cotangent):
    channels = clip.shape[-1]
    first_kernel = conv_weight.astype(jnp.float32).reshape(3, 3, 3, channels, channels)
    down_kernel = down_weight.astype(jnp.float32).reshape(3, 3, 3, channels, channels)
    clip_wide = clip.astype(jnp.float32)[None]
    pre_act = first_layer(clip_wide, first_kernel)
    activation = jax.nn.silu(pre_act).astype(jnp.bfloat16)
    outputs, down_pullback = jax.vjp(down_layer, activation.astype(jnp.float32), down_kernel)
    grad_act, grad_down = down_pullback(out_cotangent.astype(jnp.float32)[None])
    sigma = jax.nn.sigmoid(pre_act)
    grad_pre = (grad_act * sigma * (1.0 + pre_act * (1.0 - sigma))).astype(jnp.bfloat16)
    forward, first_pullback = jax.vjp(first_layer, clip_wide, first_kernel)
    grad_clip, grad_conv = first_pullback(grad_pre.astype(jnp.float32))
    return (grad_clip[0].astype(jnp.bfloat16), grad_conv.reshape(27 * channels, channels), grad_down.reshape(27 * channels, channels))
```

```python
import jax
import jax.numpy as jnp
from jax import lax
from jax.sharding import PartitionSpec as P


def from_next(x, axis):
    count = lax.axis_size(axis)
    got = lax.ppermute(x, axis, [((i + 1) % count, i) for i in range(count)])
    return jnp.where(lax.axis_index(axis) == count - 1, jnp.zeros_like(got), got)


def from_previous(x, axis):
    count = lax.axis_size(axis)
    got = lax.ppermute(x, axis, [(i, (i + 1) % count) for i in range(count)])
    return jnp.where(lax.axis_index(axis) == 0, jnp.zeros_like(got), got)


def convolve(inputs, kernel, specs, padding, lhs_step, rhs_step):
    return lax.conv_general_dilated(
        inputs,
        kernel,
        (1, 1, 1),
        padding,
        lhs_dilation=lhs_step,
        rhs_dilation=rhs_step,
        dimension_numbers=specs,
        preferred_element_type=jnp.float32,
    )


def extend(clip, cot, dim, axis):
    clip_edge = lax.slice_in_dim(clip, 0, 2, axis=dim)
    cot_edge = lax.slice_in_dim(cot, 0, 1, axis=dim)
    channels = clip.shape[-1]
    rows = clip_edge.size // channels
    packed = jnp.concatenate(
        [clip_edge.reshape(rows, channels), cot_edge.reshape(-1, channels)], axis=0
    )
    packed = from_next(packed, axis)
    return (
        jnp.concatenate([clip, packed[:rows].reshape(clip_edge.shape)], axis=dim),
        jnp.concatenate([cot, packed[rows:].reshape(cot_edge.shape)], axis=dim),
    )


def owned(axis, length):
    place, count = lax.axis_index(axis), lax.axis_size(axis)
    spot = jnp.arange(length)
    return ((spot > 0) | (place == 0)) & ((spot < length - 1) | (place < count - 1))


def local(clip, conv_weight, down_weight, out_cotangent):
    frames, rows, columns, channels = clip.shape
    ta, ha, wa = lax.axis_size("ta"), lax.axis_size("ha"), lax.axis_size("wa")
    share = channels // ta
    first_kernel = conv_weight.reshape(3, 3, 3, channels, channels)
    down_kernel = down_weight.reshape(3, 3, 3, channels, channels)
    unit = (1, 1, 1)
    forward_specs = ("NDHWC", "DHWIO", "NDHWC")
    back_specs = ("NDHWC", "DHWOI", "NDHWC")
    weight_specs = ("CDHWN", "IDHWO", "DHWNC")
    here = frames * rows * columns
    packed = jnp.concatenate(
        [clip.reshape(here, channels), out_cotangent.reshape(-1, channels)], axis=0
    )
    packed = lax.all_gather(packed, "ta", axis=0, tiled=False)
    clips = packed[:, :here].reshape(ta * frames, rows, columns, channels)
    cots = packed[:, here:].reshape((-1,) + out_cotangent.shape[1:])
    clips, cots = extend(clips, cots, 1, "ha")
    clips, cots = extend(clips, cots, 2, "wa")
    pre_act = convolve(
        clips[None], first_kernel, forward_specs, [(2, 0), (1, 0), (1, 0)], unit, unit
    )[0]
    own = (owned("ha", rows + 1)[:, None] & owned("wa", columns + 1)[None, :])[None, :, :, None]
    activation = jnp.where(own, jax.nn.silu(pre_act), 0.0).astype(jnp.bfloat16)
    flipped_down = down_kernel[::-1, ::-1, ::-1]
    grad_act = convolve(
        cots[None], flipped_down, back_specs, [(0, 3), (1, 1), (1, 1)], (2, 2, 2), unit
    )[0]
    sigma = jax.nn.sigmoid(pre_act)
    grad_pre = grad_act * sigma * (1.0 + pre_act * (1.0 - sigma))
    grad_pre = jnp.where(own, grad_pre, 0.0).astype(jnp.bfloat16)
    place = lax.axis_index("ta")
    later = jnp.pad(grad_pre, ((0, 2), (0, 0), (0, 0), (0, 0)))
    later = lax.dynamic_slice_in_dim(later, place * frames, frames + 2, 0)
    flipped_first = first_kernel[::-1, ::-1, ::-1]
    grad_clip = convolve(
        later[None], flipped_first, back_specs, [(0, 0), (1, 2), (1, 2)], unit, unit
    )[0]
    start = place * share
    cot_share = lax.dynamic_slice_in_dim(cots, start, share, 3)
    grad_share = lax.dynamic_slice_in_dim(grad_pre, start, share, 3)
    grad_down = convolve(
        activation[None, :-1], cot_share[None], weight_specs, [(2, 0), (1, 1), (1, 1)], unit, (2, 2, 2)
    )
    grad_conv = convolve(
        clips[None], grad_share[None], weight_specs, [(2, 0), (1, 0), (1, 0)], unit, unit
    )
    both = jnp.concatenate(
        [grad_conv.reshape(27 * channels, share), grad_down.reshape(27 * channels, share)], axis=1
    )
    part = 27 * channels // (ha * wa)
    both = both.reshape(ha // 2, 2, wa, part, 2 * share)
    core = lax.axis_index("ha") % 2
    mine = lax.dynamic_index_in_dim(both, core, 1, keepdims=False)
    other = lax.dynamic_index_in_dim(both, 1 - core, 1, keepdims=False).astype(jnp.bfloat16)
    other = lax.ppermute(other, "ha", [(i, i ^ 1) for i in range(ha)])
    pair = (mine + other.astype(jnp.float32)).astype(jnp.bfloat16)
    groups = [[h * wa + w for h in range(c, ha, 2) for w in range(wa)] for c in range(2)]
    pair = pair.reshape(ha * wa // 2 * part, 2 * share)
    spread = lax.all_to_all(pair, ("ha", "wa"), 0, 0, axis_index_groups=groups, tiled=True)
    total = jnp.sum(spread.reshape(ha * wa // 2, part, 2 * share).astype(jnp.float32), axis=0)
    past = from_previous(grad_clip[:, :, columns:], "wa")
    grad_clip = grad_clip[:, :, :columns]
    grad_clip = grad_clip.at[:, :, :2].add(past)
    past = from_previous(grad_clip[:, rows:], "ha")
    grad_clip = grad_clip[:, :rows].at[:, :2].add(past)
    return (grad_clip.astype(jnp.bfloat16), total[:, :share], total[:, share:])


def solution(mesh):
    return jax.shard_map(
        local,
        mesh=mesh,
        in_specs=(P("ta", "ha", "wa", None), P(), P(), P("ta", "ha", "wa", None)),
        out_specs=(P("ta", "ha", "wa", None), P(("ha", "wa"), "ta"), P(("ha", "wa"), "ta")),
        check_vma=False,
    )
```

```python
import jax
import jax.numpy as jnp
from jax import lax
from jax.experimental import pallas as pl
from jax.experimental.pallas import tpu as pltpu
from jax.sharding import PartitionSpec as P

F, R, W, C = 2, 4, 16, 256
TA, HA, WA = 4, 8, 8
T = TA * F
HEAD = 2 * F * W + (R // 2) * (W // 2)
BLOCK = F * R * W + (R // 2) * (W // 2)
SHARE = C // TA
PART = 27 * C // (HA * WA)
SLOT = 112
PEERS = HA * WA // 2
TAPS = [(a, b, c) for a in range(3) for b in range(3) for c in range(3)]
BF16, F32 = jnp.bfloat16, jnp.float32
VMEM_BYTES = 48 * 1024 * 1024


def iota(shape, dim):
    return lax.broadcasted_iota(jnp.int32, shape, dim)


def onehot(hit):
    return jnp.where(hit, 1.0, 0.0).astype(F32).astype(BF16)


def dot(x, y):
    return jnp.dot(x, y, preferred_element_type=F32)


def dot_t(x, y):
    return lax.dot_general(x, y, (((1,), (1,)), ((), ())), preferred_element_type=F32)


def column(order):
    return jnp.where(order < W // 2, 2 * order, 2 * (order - W // 2) + 1)


def frame_rows(g_ref, h_ref, t):
    s, f = t // F, t % F
    low = 2 * W * f
    return [
        g_ref[s, low : low + 2 * W],
        g_ref[s, HEAD + low : HEAD + low + 2 * W],
        h_ref[s, low : low + 2 * W],
    ]


def edge_kernel(g_ref, h_ref, out_ref):
    cot = 2 * F * W
    m, n = iota((16, 128), 0), iota((16, 128), 1)
    source = jnp.where(m < 12, (m // 2) * W + m % 2, jnp.where(m < 14, 96 + (m - 12) * 8, 112))
    pick = onehot((n == source) & (m < 15))
    for t in range(T):
        s = t // F
        rows = frame_rows(g_ref, h_ref, t) + [g_ref[s, cot : cot + 16], h_ref[s, cot : cot + 16]]
        out_ref[t] = dot(pick, jnp.concatenate(rows, axis=0)).astype(BF16)


def main_kernel(
    at_ref, g_ref, h_ref, w_ref, k1_ref, kd_ref, mine_ref, other_ref, later_ref,
    k1, kd, xb, cu, pre, act, gp, tt, sem1, semd,
):
    ta, last_h, last_w = at_ref[0], at_ref[1] == HA - 1, at_ref[2] == WA - 1
    core = lax.rem(at_ref[1], 2)
    cot = 2 * F * W
    step = 3 * C
    copies1 = [
        pltpu.make_async_copy(k1_ref.at[pl.ds(i * step, step)], k1.at[pl.ds(i * step, step)], sem1.at[i])
        for i in range(9)
    ]
    copiesd = [
        pltpu.make_async_copy(kd_ref.at[pl.ds(i * step, step)], kd.at[pl.ds(i * step, step)], semd.at[i])
        for i in range(9)
    ]
    for copy in copies1 + copiesd:
        copy.start()

    m, n = iota((576, 112), 0), iota((576, 112), 1)
    tap, place = m // 64, m % 64
    b, c, k, col = tap // 3, tap % 3, place // W, column(place % W)
    row, v = k + b, col + c
    source = jnp.where(v < W, row * W + v, 96 + row * 2 + v - W)
    out_h = last_h & (((b == 0) & (k == 3)) | ((b == 2) & (k == 2)))
    out_w = last_w & (((c == 0) & (col == 15)) | ((c == 2) & (col == 14)))
    pick = onehot((n == source) & jnp.logical_not(out_h | out_w))
    for i in range(9):
        xb[i, 0:2] = jnp.zeros((2, 64, C), BF16)
    for t in range(T):
        rows = jnp.concatenate(frame_rows(g_ref, h_ref, t) + [w_ref[t]], axis=0)
        built = dot(pick, rows).astype(BF16)
        for i in range(9):
            xb[i, t + 2] = built[i * 64 : (i + 1) * 64]

    m, n = iota((144, 48), 0), iota((144, 48), 1)
    tap, place = m // 16, m % 16
    b, c, kk, mm = tap // 3, tap % 3, place // 8, place % 8
    r, q = kk + jnp.where(b < 2, 1, 0), mm + jnp.where(c < 2, 1, 0)
    source = jnp.where(q == 8, 44 + r, r * 8 + q)
    out_h = last_h & (b == 0) & (kk == 1)
    out_w = last_w & (c == 0) & (mm == 7)
    pick = onehot((n == source) & jnp.logical_not(out_h | out_w))
    for i in range(9):
        cu[i, TA] = jnp.zeros((16, C), BF16)
    for j in range(TA):
        rows = jnp.concatenate(
            [g_ref[j, cot : cot + 16], h_ref[j, cot : cot + 16], w_ref[2 * j]], axis=0
        )
        built = dot(pick, rows).astype(BF16)
        for i in range(9):
            cu[i, j] = built[i * 16 : (i + 1) * 16]

    for i, (a, b, c) in enumerate(TAPS):
        if i % 3 == 0:
            copies1[i // 3].wait()
        x = xb[b * 3 + c, a : a + T].reshape(T * 64, C)
        y = dot(x, k1[i * C : (i + 1) * C])
        if i == 0:
            pre[...] = y
        else:
            pre[...] += y

    for copy in copiesd:
        copy.wait()
    for te in range(2):
        for ke in range(2):
            for ce in range(2):
                total = None
                for i, (a, b, c) in enumerate(TAPS):
                    if (a == 1, b == 1, c == 1) != (te == 1, ke == 1, ce == 1):
                        continue
                    ja = 1 if a < 2 else 0
                    y = dot_t(cu[b * 3 + c, ja : ja + 4].reshape(64, C), kd[i * C : (i + 1) * C])
                    total = y if total is None else total + y
                for j in range(4):
                    for kk in range(2):
                        t, k = 2 * j + te, 2 * kk + ke
                        spot = t * 64 + k * W + ce * 8
                        x = pre[spot : spot + 8]
                        s = 1.0 / (1.0 + jnp.exp(-x))
                        at = (j * 2 + kk) * 8
                        g = total[at : at + 8]
                        act[te * 4 + ke * 2 + ce, at : at + 8] = x * s
                        pre[spot : spot + 8] = g * s * (1.0 + x * (1.0 - s))
    gp[0:2] = jnp.zeros((2, 64, C), BF16)
    gp[2 : T + 2] = pre[...].astype(BF16).reshape(T, 64, C)
    gp[T + 2 : T + 4] = jnp.zeros((2, 64, C), BF16)
    later_ref[...] = gp[pl.ds(2 + F * ta, F + 2)]

    share = onehot(iota((SHARE, C), 1) == iota((SHARE, C), 0) + ta * SHARE)
    left = jnp.concatenate(
        [
            dot_t(share, gp[2 - a : 2 - a + T + 2].reshape((T + 2) * 64, C)).astype(BF16)
            for a in range(3)
        ],
        axis=0,
    )
    for bc in range(9):
        y = dot(left, xb[bc].reshape((T + 2) * 64, C)).astype(BF16)
        for a in range(3):
            tt[a * 9 + bc, 0:SHARE] = y[a * SHARE : (a + 1) * SHARE]
    for bc in range(9):
        for ja in range(2):
            cots = dot_t(share, cu[bc, ja : ja + 4].reshape(64, C)).astype(BF16)
            for a in (0, 1) if ja == 1 else (2,):
                kind = (4 if a == 1 else 0) + (2 if bc // 3 == 1 else 0) + (1 if bc % 3 == 1 else 0)
                tt[a * 9 + bc, SHARE:] = dot(cots, act[kind].astype(BF16)).astype(BF16)

    m, n = iota((SLOT, C), 0), iota((SLOT, C), 1)
    for x in range(HA // 2):
        for w in range(WA):
            pair = []
            for cc in range(2):
                first = ((x * 2 + cc) * WA + w) * PART
                tap, off = first // C, first % C
                y = dot_t(onehot((n == m + off) & (m < PART)), tt[tap])
                if off + PART > C:
                    y += dot_t(onehot((n == m + off - C) & (m < PART)), tt[tap + 1])
                pair.append(y)
            spot = (x * WA + w) * SLOT
            mine_ref[spot : spot + SLOT] = jnp.where(core == 0, pair[0], pair[1]).astype(BF16)
            other_ref[spot : spot + SLOT] = jnp.where(core == 0, pair[1], pair[0]).astype(BF16)


WIDE = 144


def clip_kernel(at_ref, later_ref, k1_ref, main_ref, spill_ref, k1, yb, acc, sem):
    last_h, last_w = at_ref[1] == HA - 1, at_ref[2] == WA - 1
    step = 3 * C
    copies = [
        pltpu.make_async_copy(k1_ref.at[pl.ds(i * step, step)], k1.at[pl.ds(i * step, step)], sem.at[i])
        for i in range(9)
    ]
    for copy in copies:
        copy.start()
    for i in range(9):
        b, c = i // 3, i % 3
        m, n = iota((WIDE, 64), 0), iota((WIDE, 64), 1)
        past = m >= 96
        h = jnp.where(past, (m - 96) // 8, m // W)
        v = jnp.where(past, W + (m - 96) % 8, m % W)
        k, col = n // W, column(n % W)
        hit = (h == k + b) & (v == col + c) & (v < W + 2)
        if b != 1:
            hit = hit & jnp.logical_not(last_h & (k == (3 if b == 0 else 2)))
        if c != 1:
            hit = hit & jnp.logical_not(last_w & (col == (15 if c == 0 else 14)))
        pick = onehot(hit)
        for t in range(F + 2):
            yb[i, t] = dot(pick, later_ref[t]).astype(BF16)
    for i, (a, b, c) in enumerate(TAPS):
        if i % 3 == 0:
            copies[i // 3].wait()
        y = dot_t(yb[b * 3 + c, 2 - a : 2 - a + F].reshape(F * WIDE, C), k1[i * C : (i + 1) * C])
        if i == 0:
            acc[...] = y
        else:
            acc[...] += y
    for f in range(F):
        main_ref[f] = acc[f * WIDE : f * WIDE + 96]
        spill_ref[f] = acc[f * WIDE + 96 : (f + 1) * WIDE]


def sum_kernel(parts_ref, conv_ref, down_ref):
    total = parts_ref[0].astype(F32)
    for i in range(1, PEERS):
        total += parts_ref[i].astype(F32)
    conv_ref[...] = total[:PART, :SHARE]
    down_ref[...] = total[:PART, SHARE:]


def whole():
    return pl.BlockSpec(memory_space=pltpu.VMEM)


def call(kernel, outs, specs, scratch, flops, name):
    return pl.pallas_call(
        kernel,
        out_shape=outs,
        in_specs=specs,
        out_specs=jax.tree.map(lambda _: whole(), outs),
        scratch_shapes=scratch,
        compiler_params=pltpu.CompilerParams(vmem_limit_bytes=VMEM_BYTES),
        cost_estimate=pl.CostEstimate(flops=flops, bytes_accessed=8_000_000, transcendentals=0),
        name=name,
    )


def shape(dims, dtype=BF16):
    return jax.ShapeDtypeStruct(dims, dtype)


def shift(x, axis, by):
    count = lax.axis_size(axis)
    return lax.ppermute(x, axis, [(i, (i + by) % count) for i in range(count)])


def local(clip, conv_weight, down_weight, out_cotangent):
    smem, anywhere = pl.BlockSpec(memory_space=pltpu.SMEM), pl.BlockSpec(memory_space=pl.ANY)
    at = jnp.stack([lax.axis_index(a) for a in ("ta", "ha", "wa")]).astype(jnp.int32)
    head = clip[:, :2].reshape(2 * F * W, C)
    tail = clip[:, 2:].reshape(2 * F * W, C)
    packed = jnp.concatenate([head, out_cotangent.reshape(-1, C), tail], axis=0)
    g = lax.all_gather(packed, "ta", axis=0, tiled=False)
    h = shift(g[:, :HEAD], "ha", -1)
    w = call(edge_kernel, shape((T, 16, C)), [whole()] * 2, [], 10**7, "edge")(g, h)
    w = shift(w, "wa", -1)
    mine, other, later = call(
        main_kernel,
        [shape((PEERS * SLOT, 2 * SHARE)), shape((PEERS * SLOT, 2 * SHARE)), shape((F + 2, 64, C))],
        [smem, whole(), whole(), whole(), anywhere, anywhere],
        [
            pltpu.VMEM((27 * C, C), BF16),
            pltpu.VMEM((27 * C, C), BF16),
            pltpu.VMEM((9, T + 2, 64, C), BF16),
            pltpu.VMEM((9, TA + 1, 16, C), BF16),
            pltpu.VMEM((T * 64, C), F32),
            pltpu.VMEM((8, 64, C), F32),
            pltpu.VMEM((T + 4, 64, C), BF16),
            pltpu.VMEM((27, 2 * SHARE, C), BF16),
            pltpu.SemaphoreType.DMA((9,)),
            pltpu.SemaphoreType.DMA((9,)),
        ],
        5 * 10**9,
        "main",
    )(at, g, h, w, conv_weight, down_weight)
    other = lax.ppermute(other, "ha", [(i, i ^ 1) for i in range(HA)])
    grad_clip, spill = call(
        clip_kernel,
        [shape((F, 96, C), F32), shape((F, 48, C), F32)],
        [smem, whole(), anywhere],
        [
            pltpu.VMEM((27 * C, C), BF16),
            pltpu.VMEM((9, F + 2, WIDE, C), BF16),
            pltpu.VMEM((F * WIDE, C), F32),
            pltpu.SemaphoreType.DMA((9,)),
        ],
        10**9,
        "clip",
    )(at, later, conv_weight)
    spill = shift(spill, "wa", 1)
    pair = (mine.astype(F32) + other.astype(F32)).astype(BF16)
    groups = [[i * WA + w for i in range(c, HA, 2) for w in range(WA)] for c in range(2)]
    parts = lax.all_to_all(pair, ("ha", "wa"), 0, 0, axis_index_groups=groups, tiled=True)
    grad_conv, grad_down = call(
        sum_kernel, [shape((PART, SHARE), F32), shape((PART, SHARE), F32)], [whole()], [], 10**6, "sum"
    )(parts.reshape(PEERS, SLOT, 2 * SHARE))
    grad_clip = grad_clip.reshape(F, 6, W, C)
    spill = spill.reshape(F, 6, 8, C)
    grad_clip = jnp.concatenate([grad_clip[:, :, :8] + spill, grad_clip[:, :, 8:]], axis=2)
    past = shift(grad_clip[:, R:], "ha", 1)
    grad_clip = jnp.concatenate([grad_clip[:, :2] + past, grad_clip[:, 2:R]], axis=1).astype(BF16)
    return (grad_clip, grad_conv, grad_down)


def solution(mesh):
    return jax.shard_map(
        local,
        mesh=mesh,
        in_specs=(P("ta", "ha", "wa", None), P(), P(), P("ta", "ha", "wa", None)),
        out_specs=(P("ta", "ha", "wa", None), P(("ha", "wa"), "ta"), P(("ha", "wa"), "ta")),
        check_vma=False,
    )
```

```python
import jax
import jax.numpy as jnp
from jax import lax
from jax.experimental import pallas as pl
from jax.experimental.pallas import tpu as pltpu
from jax.sharding import PartitionSpec as P

F, R, W, C = 2, 4, 16, 256
TA, HA, WA = 4, 8, 8
T = TA * F
HEAD = 2 * F * W + (R // 2) * (W // 2)
BLOCK = F * R * W + (R // 2) * (W // 2)
SHARE = C // TA
PART = 27 * C // (HA * WA)
SLOT = 112
PEERS = HA * WA // 2
TAPS = [(a, b, c) for a in range(3) for b in range(3) for c in range(3)]
BF16, F32 = jnp.bfloat16, jnp.float32
VMEM_BYTES = 28 * 1024 * 1024


def iota(shape, dim):
    return lax.broadcasted_iota(jnp.int32, shape, dim)


def onehot(hit):
    return jnp.where(hit, 1.0, 0.0).astype(F32).astype(BF16)


def dot(x, y):
    return jnp.dot(x, y, preferred_element_type=F32)


def dot_t(x, y):
    return lax.dot_general(x, y, (((1,), (1,)), ((), ())), preferred_element_type=F32)


def column(order):
    return jnp.where(order < W // 2, 2 * order, 2 * (order - W // 2) + 1)


def frame_rows(g_ref, h_ref, t):
    s, f = t // F, t % F
    low = 2 * W * f
    return [
        g_ref[s, low : low + 2 * W],
        g_ref[s, HEAD + low : HEAD + low + 2 * W],
        h_ref[s, low : low + 2 * W],
    ]


def edge_kernel(g_ref, h_ref, out_ref):
    cot = 2 * F * W
    m, n = iota((16, 128), 0), iota((16, 128), 1)
    source = jnp.where(m < 12, (m // 2) * W + m % 2, jnp.where(m < 14, 96 + (m - 12) * 8, 112))
    pick = onehot((n == source) & (m < 15))
    for t in range(T):
        s = t // F
        rows = frame_rows(g_ref, h_ref, t) + [g_ref[s, cot : cot + 16], h_ref[s, cot : cot + 16]]
        out_ref[t] = dot(pick, jnp.concatenate(rows, axis=0)).astype(BF16)


def pack_kernel(clip_ref, cot_ref, out_ref, sems):
    half = 2 * W
    copies = []
    for f in range(F):
        for part in range(2):
            for k in range(2):
                spot = part * HEAD + f * half + k * W
                copies.append((clip_ref.at[f, 2 * part + k], out_ref.at[pl.ds(spot, W)]))
    copies.append((cot_ref, out_ref.at[pl.ds(2 * F * W, 16)]))
    copies = [pltpu.make_async_copy(x, y, sems.at[i]) for i, (x, y) in enumerate(copies)]
    for copy in copies:
        copy.start()
    for copy in copies:
        copy.wait()


TABLE = 2 * C // 4 + C + SLOT


def load_kernel(at_ref, after_ref, k1_ref, kd_ref, k1, kd, table_ref, sems):
    step = 3 * C
    copies = []
    for x, y in ((k1_ref, k1), (kd_ref, kd)):
        for i in range(9):
            part = pl.ds(i * step, step)
            copies.append(pltpu.make_async_copy(x.at[part], y.at[part], sems.at[len(copies)]))
    for copy in copies:
        copy.start()
    m, n = iota((TABLE, C), 0), iota((TABLE, C), 1)
    for r in range(4):
        table_ref[r] = onehot(n == m + (4 * r - C // 2))
    for copy in copies:
        copy.wait()


def window_pick(at_ref):
    last_h, last_w = at_ref[1] == HA - 1, at_ref[2] == WA - 1
    m, n = iota((576, 112), 0), iota((576, 112), 1)
    tap, place = m // 64, m % 64
    b, c, k, col = tap // 3, tap % 3, place // W, column(place % W)
    row, v = k + b, col + c
    source = jnp.where(v < W, row * W + v, 96 + row * 2 + v - W)
    out_h = last_h & (((b == 0) & (k == 3)) | ((b == 2) & (k == 2)))
    out_w = last_w & (((c == 0) & (col == 15)) | ((c == 2) & (col == 14)))
    return onehot((n == source) & jnp.logical_not(out_h | out_w))


def early_kernel(at_ref, g_ref, h_ref, k1, xb, pre, edge_ref):
    pick = window_pick(at_ref)
    edge_ref[...] = pick[:, 96:]
    own = pick[:, :96]
    for i in range(9):
        xb[i, 0:2] = jnp.zeros((2, 64, C), BF16)
    for t in range(T):
        built = dot(own, jnp.concatenate(frame_rows(g_ref, h_ref, t), axis=0)).astype(BF16)
        for i in range(9):
            xb[i, t + 2] = built[i * 64 : (i + 1) * 64]
    for i, (a, b, c) in enumerate(TAPS):
        y = dot(xb[b * 3 + c, a : a + T].reshape(T * 64, C), k1[i * C : (i + 1) * C])
        if i == 0:
            pre[...] = y
        else:
            pre[...] += y


def main_kernel(
    at_ref, g_ref, h_ref, w_ref, k1, kd, table_ref, xb_ref, pre_ref, edge_ref,
    mine_ref, other_ref, later_ref, xb, cu, pre, act, gp, tt, fix,
):
    ta, last_h, last_w = at_ref[0], at_ref[1] == HA - 1, at_ref[2] == WA - 1
    core = lax.rem(at_ref[1], 2)
    cot = 2 * F * W

    edges = w_ref[...].reshape(T * 16, C)
    m, n = iota((64, T * 16), 0), iota((64, T * 16), 1)
    t, k, e = m // 8, (m // 2) % 4, m % 2
    total = None
    for i, (a, b, c) in enumerate(TAPS):
        if c == 0:
            continue
        hit = (n == (t - 2 + a) * 16 + (k + b) * 2 + e + (c - 2)) & (e + c >= 2)
        if b != 1:
            hit = hit & jnp.logical_not(last_h & (k == (3 if b == 0 else 2)))
        if c == 2:
            hit = hit & jnp.logical_not(last_w & (e == 0))
        y = dot(dot(onehot(hit), edges).astype(BF16), k1[i * C : (i + 1) * C])
        total = y if total is None else total + y
    fix[...] = total

    m, n = iota((144, 48), 0), iota((144, 48), 1)
    tap, place = m // 16, m % 16
    b, c, kk, mm = tap // 3, tap % 3, place // 8, place % 8
    r, q = kk + jnp.where(b < 2, 1, 0), mm + jnp.where(c < 2, 1, 0)
    source = jnp.where(q == 8, 44 + r, r * 8 + q)
    out_h = last_h & (b == 0) & (kk == 1)
    out_w = last_w & (c == 0) & (mm == 7)
    pick = onehot((n == source) & jnp.logical_not(out_h | out_w))
    for i in range(9):
        cu[i, TA] = jnp.zeros((16, C), BF16)
    for j in range(TA):
        rows = jnp.concatenate(
            [g_ref[j, cot : cot + 16], h_ref[j, cot : cot + 16], w_ref[2 * j]], axis=0
        )
        built = dot(pick, rows).astype(BF16)
        for i in range(9):
            cu[i, j] = built[i * 16 : (i + 1) * 16]

    last = iota((8, C), 0) == 7
    for te in range(2):
        for ke in range(2):
            for ce in range(2):
                total = None
                for i, (a, b, c) in enumerate(TAPS):
                    if (a == 1, b == 1, c == 1) != (te == 1, ke == 1, ce == 1):
                        continue
                    ja = 1 if a < 2 else 0
                    y = dot_t(cu[b * 3 + c, ja : ja + 4].reshape(64, C), kd[i * C : (i + 1) * C])
                    total = y if total is None else total + y
                for j in range(4):
                    for kk in range(2):
                        t, k = 2 * j + te, 2 * kk + ke
                        spot = t * 64 + k * W + ce * 8
                        late = (t * 4 + k) * 2 + ce
                        x = pre_ref[spot : spot + 8] + jnp.where(last, fix[late : late + 1], 0.0)
                        s = 1.0 / (1.0 + jnp.exp(-x))
                        at = (j * 2 + kk) * 8
                        g = total[at : at + 8]
                        act[te * 4 + ke * 2 + ce, at : at + 8] = x * s
                        pre[spot : spot + 8] = g * s * (1.0 + x * (1.0 - s))
    gp[0:2] = jnp.zeros((2, 64, C), BF16)
    gp[2 : T + 2] = pre[...].astype(BF16).reshape(T, 64, C)
    gp[T + 2 : T + 4] = jnp.zeros((2, 64, C), BF16)
    later_ref[...] = gp[pl.ds(2 + F * ta, F + 2)]

    share = onehot(iota((SHARE, C), 1) == iota((SHARE, C), 0) + ta * SHARE)
    left = jnp.concatenate(
        [
            dot_t(share, gp[2 - a : 2 - a + T + 2].reshape((T + 2) * 64, C)).astype(BF16)
            for a in range(3)
        ],
        axis=0,
    )
    late = edge_ref[...]
    for bc in range(9):
        xb[bc, 0:2] = jnp.zeros((2, 64, C), BF16)
    for t in range(T):
        built = dot(late, w_ref[t]).astype(BF16)
        for bc in range(9):
            xb[bc, t + 2] = xb_ref[bc, t + 2] + built[bc * 64 : (bc + 1) * 64]
    for bc in range(9):
        y = dot(left, xb[bc].reshape((T + 2) * 64, C)).astype(BF16)
        for a in range(3):
            tt[a * 9 + bc, 0:SHARE] = y[a * SHARE : (a + 1) * SHARE]
    cots = {}
    for bc in range(9):
        for ja in range(2):
            cots[bc, ja] = dot_t(share, cu[bc, ja : ja + 4].reshape(64, C)).astype(BF16)
    for kind in range(8):
        taps = [
            (i, cots[b * 3 + c, 1 if a < 2 else 0])
            for i, (a, b, c) in enumerate(TAPS)
            if (a == 1) * 4 + (b == 1) * 2 + (c == 1) == kind
        ]
        y = dot(jnp.concatenate([x for _, x in taps], axis=0), act[kind].astype(BF16)).astype(BF16)
        for place, (i, _) in enumerate(taps):
            tt[i, SHARE:] = y[place * SHARE : (place + 1) * SHARE]

    for x in range(HA // 2):
        for w in range(WA):
            pair = []
            for cc in range(2):
                first = ((x * 2 + cc) * WA + w) * PART
                tap, off = first // C, first % C
                r, low = off % 16 // 4, off // 16 * 16 + C // 2
                y = dot_t(table_ref[r, low : low + SLOT], tt[tap])
                if off + PART > C:
                    y += dot_t(table_ref[r, low - C : low - C + SLOT], tt[tap + 1])
                pair.append(y)
            spot = (x * WA + w) * SLOT
            mine_ref[spot : spot + SLOT] = jnp.where(core == 0, pair[0], pair[1]).astype(BF16)
            other_ref[spot : spot + SLOT] = jnp.where(core == 0, pair[1], pair[0]).astype(BF16)


WIDE = 144


def clip_kernel(at_ref, later_ref, k1, main_ref, spill_ref, yb, acc):
    last_h, last_w = at_ref[1] == HA - 1, at_ref[2] == WA - 1
    for i in range(9):
        b, c = i // 3, i % 3
        m, n = iota((WIDE, 64), 0), iota((WIDE, 64), 1)
        past = m >= 96
        h = jnp.where(past, (m - 96) // 8, m // W)
        v = jnp.where(past, W + (m - 96) % 8, m % W)
        k, col = n // W, column(n % W)
        hit = (h == k + b) & (v == col + c) & (v < W + 2)
        if b != 1:
            hit = hit & jnp.logical_not(last_h & (k == (3 if b == 0 else 2)))
        if c != 1:
            hit = hit & jnp.logical_not(last_w & (col == (15 if c == 0 else 14)))
        pick = onehot(hit)
        for t in range(F + 2):
            yb[i, t] = dot(pick, later_ref[t]).astype(BF16)
    for i, (a, b, c) in enumerate(TAPS):
        y = dot_t(yb[b * 3 + c, 2 - a : 2 - a + F].reshape(F * WIDE, C), k1[i * C : (i + 1) * C])
        if i == 0:
            acc[...] = y
        else:
            acc[...] += y
    for f in range(F):
        main_ref[f] = acc[f * WIDE : f * WIDE + 96]
        spill_ref[f] = acc[f * WIDE + 96 : (f + 1) * WIDE]


def join_kernel(mine_ref, other_ref, after_ref, out_ref):
    out_ref[...] = (mine_ref[...].astype(F32) + other_ref[...].astype(F32)).astype(BF16)


def sum_kernel(parts_ref, conv_ref, down_ref):
    total = parts_ref[0].astype(F32)
    for i in range(1, PEERS):
        total += parts_ref[i].astype(F32)
    total = jnp.concatenate([total, jnp.zeros((128 - SLOT, 2 * SHARE), F32)], axis=0).T
    conv_ref[...] = total[:SHARE, :PART]
    down_ref[...] = total[SHARE:, :PART]


def whole():
    return pl.BlockSpec(memory_space=pltpu.VMEM)


def call(kernel, outs, specs, scratch, flops, name):
    return pl.pallas_call(
        kernel,
        out_shape=outs,
        in_specs=specs,
        out_specs=jax.tree.map(lambda _: whole(), outs),
        scratch_shapes=scratch,
        compiler_params=pltpu.CompilerParams(vmem_limit_bytes=VMEM_BYTES),
        cost_estimate=pl.CostEstimate(flops=flops, bytes_accessed=8_000_000, transcendentals=0),
        name=name,
    )


def shape(dims, dtype=BF16):
    return jax.ShapeDtypeStruct(dims, dtype)


def on_chip(dims, dtype=BF16):
    return pltpu.VMEM(dims, dtype)


def in_hbm(x):
    return pltpu.with_memory_space_constraint(x, pltpu.HBM)


def in_vmem(x):
    return pltpu.with_memory_space_constraint(x, pltpu.VMEM)


def shift(x, axis, by):
    count = lax.axis_size(axis)
    return lax.ppermute(x, axis, [(i, (i + by) % count) for i in range(count)])


def local(clip, conv_weight, down_weight, out_cotangent):
    smem, anywhere = pl.BlockSpec(memory_space=pltpu.SMEM), pl.BlockSpec(memory_space=pl.ANY)
    at = jnp.stack([lax.axis_index(a) for a in ("ta", "ha", "wa")]).astype(jnp.int32)
    dma = pltpu.SemaphoreType.DMA
    packed = call(
        pack_kernel, shape((BLOCK, C)), [anywhere] * 2, [dma((9,))], 10**5, "pack"
    )(in_hbm(clip), in_hbm(out_cotangent.reshape(-1, C)))
    g = lax.all_gather(packed, "ta", axis=0, tiled=False)
    h = shift(g[:, :HEAD], "ha", -1)
    weight = on_chip((27 * C, C))
    k1, kd, table = call(
        load_kernel,
        [weight, weight, on_chip((4, TABLE, C))],
        [smem] + [anywhere] * 3,
        [dma((18,))],
        3 * 10**9,
        "load",
    )(at, g, in_hbm(conv_weight), in_hbm(down_weight))
    k1, kd, table = in_vmem(k1), in_vmem(kd), in_vmem(table)
    w = call(edge_kernel, shape((T, 16, C)), [whole()] * 2, [], 10**7, "edge")(g, h)
    w = shift(w, "wa", -1)
    xb, pre, edge = call(
        early_kernel,
        [shape((9, T + 2, 64, C)), shape((T * 64, C), F32), shape((576, 16))],
        [smem] + [whole()] * 3,
        [],
        4 * 10**9,
        "early",
    )(at, g, h, k1)
    mine, other, later = call(
        main_kernel,
        [shape((PEERS * SLOT, 2 * SHARE)), shape((PEERS * SLOT, 2 * SHARE)), shape((F + 2, 64, C))],
        [smem] + [whole()] * 9,
        [
            pltpu.VMEM((9, T + 2, 64, C), BF16),
            pltpu.VMEM((9, TA + 1, 16, C), BF16),
            pltpu.VMEM((T * 64, C), F32),
            pltpu.VMEM((8, 64, C), F32),
            pltpu.VMEM((T + 4, 64, C), BF16),
            pltpu.VMEM((27, 2 * SHARE, C), BF16),
            pltpu.VMEM((64, C), F32),
        ],
        5 * 10**9,
        "main",
    )(at, g, h, w, k1, kd, table, xb, pre, edge)
    other = lax.ppermute(other, "ha", [(i, i ^ 1) for i in range(HA)])
    grad_clip, spill = call(
        clip_kernel,
        [shape((F, 96, C), F32), shape((F, 48, C), F32)],
        [smem, whole(), whole()],
        [pltpu.VMEM((9, F + 2, WIDE, C), BF16), pltpu.VMEM((F * WIDE, C), F32)],
        10**9,
        "clip",
    )(at, later, k1)
    pair = call(
        join_kernel,
        shape((PEERS * SLOT, 2 * SHARE)),
        [whole(), whole(), anywhere],
        [],
        10**6,
        "join",
    )(mine, other, spill)
    spill = shift(spill, "wa", 1)
    groups = [[i * WA + w for i in range(c, HA, 2) for w in range(WA)] for c in range(2)]
    parts = lax.all_to_all(pair, ("ha", "wa"), 0, 0, axis_index_groups=groups, tiled=True)
    grad_conv, grad_down = call(
        sum_kernel, [shape((SHARE, PART), F32)] * 2, [whole()], [], 10**6, "sum"
    )(parts.reshape(PEERS, SLOT, 2 * SHARE))
    grad_clip = grad_clip.reshape(F, 6, W, C)
    spill = spill.reshape(F, 6, 8, C)
    grad_clip = jnp.concatenate([grad_clip[:, :, :8] + spill, grad_clip[:, :, 8:]], axis=2)
    past = shift(grad_clip[:, R:], "ha", 1)
    grad_clip = jnp.concatenate([grad_clip[:, :2] + past, grad_clip[:, 2:R]], axis=1).astype(BF16)
    return (grad_clip, grad_conv.T, grad_down.T)


def solution(mesh):
    return jax.shard_map(
        local,
        mesh=mesh,
        in_specs=(P("ta", "ha", "wa", None), P(), P(), P("ta", "ha", "wa", None)),
        out_specs=(P("ta", "ha", "wa", None), P(("ha", "wa"), "ta"), P(("ha", "wa"), "ta")),
        check_vma=False,
    )
```

```python
import jax
import jax.numpy as jnp
from jax import lax
from jax.experimental import pallas as pl
from jax.experimental.pallas import tpu as pltpu
from jax.sharding import PartitionSpec as P

F, R, W, C = 2, 4, 16, 256
TA, HA, WA = 4, 8, 8
T = TA * F
HEAD = 2 * F * W + (R // 2) * (W // 2)
BLOCK = F * R * W + (R // 2) * (W // 2)
SHARE = C // TA
PART = 27 * C // (HA * WA)
SLOT = 112
PEERS = HA * WA // 2
TAPS = [(a, b, c) for a in range(3) for b in range(3) for c in range(3)]
BF16, F32 = jnp.bfloat16, jnp.float32
VMEM_BYTES = 28 * 1024 * 1024


def iota(shape, dim):
    return lax.broadcasted_iota(jnp.int32, shape, dim)


def onehot(hit):
    return jnp.where(hit, 1.0, 0.0).astype(F32).astype(BF16)


def div(x, n):
    return lax.shift_right_logical(x, n.bit_length() - 1)


def mod(x, n):
    return lax.bitwise_and(x, n - 1)


def third(x):
    high = jnp.where(x >= 3, 1, 0) + jnp.where(x >= 6, 1, 0)
    return high, x - 3 * high


def dot(x, y):
    return jnp.dot(x, y, preferred_element_type=F32)


def dot_t(x, y):
    return lax.dot_general(x, y, (((1,), (1,)), ((), ())), preferred_element_type=F32)


def column(order):
    return jnp.where(order < W // 2, 2 * order, 2 * (order - W // 2) + 1)


def frame_rows(g_ref, h_ref, t):
    s, f = t // F, t % F
    low = 2 * W * f
    return [
        g_ref[s, low : low + 2 * W],
        g_ref[s, HEAD + low : HEAD + low + 2 * W],
        h_ref[s, low : low + 2 * W],
    ]


def edge_kernel(g_ref, h_ref, out_ref):
    cot = 2 * F * W
    m, n = iota((16, 128), 0), iota((16, 128), 1)
    source = jnp.where(m < 12, div(m, 2) * W + mod(m, 2), jnp.where(m < 14, 96 + (m - 12) * 8, 112))
    pick = onehot((n == source) & (m < 15))
    for t in range(T):
        s = t // F
        rows = frame_rows(g_ref, h_ref, t) + [g_ref[s, cot : cot + 16], h_ref[s, cot : cot + 16]]
        out_ref[t] = dot(pick, jnp.concatenate(rows, axis=0)).astype(BF16)


def pack_kernel(clip_ref, cot_ref, out_ref, sems):
    half = 2 * W
    copies = []
    for f in range(F):
        for part in range(2):
            for k in range(2):
                spot = part * HEAD + f * half + k * W
                copies.append((clip_ref.at[f, 2 * part + k], out_ref.at[pl.ds(spot, W)]))
    copies.append((cot_ref, out_ref.at[pl.ds(2 * F * W, 16)]))
    copies = [pltpu.make_async_copy(x, y, sems.at[i]) for i, (x, y) in enumerate(copies)]
    for copy in copies:
        copy.start()
    for copy in copies:
        copy.wait()


def head_kernel(at_ref, own_ref, one_ref, two_ref, three_ref, after_ref, head_ref):
    for back, ref in enumerate((own_ref, one_ref, two_ref, three_ref)):
        head_ref[lax.rem(at_ref[0] + TA - back, TA)] = ref[:HEAD]


def fetch(source, target, sems):
    step = 3 * C
    parts = [pl.ds(i * step, step) for i in range(9)]
    copies = [
        pltpu.make_async_copy(source.at[part], target.at[part], sems.at[i])
        for i, part in enumerate(parts)
    ]
    for copy in copies:
        copy.start()
    return copies


def turn(copies, plain, turned):
    for i in range(27):
        if i % 3 == 0:
            copies[i // 3].wait()
        turned[i * C : (i + 1) * C] = plain[i * C : (i + 1) * C].T


def load_kernel(at_ref, after_ref, k1_ref, k1, k1t, sems):
    turn(fetch(k1_ref, k1, sems), k1, k1t)


def window_pick(at_ref, b):
    last_h, last_w = at_ref[1] == HA - 1, at_ref[2] == WA - 1
    m, n = iota((192, 112), 0), iota((192, 112), 1)
    c, place = div(m, 64), mod(m, 64)
    k, col = div(place, W), column(mod(place, W))
    row, v = k + b, col + c
    source = jnp.where(v < W, row * W + v, 96 + row * 2 + v - W)
    out = last_w & (((c == 0) & (col == 15)) | ((c == 2) & (col == 14)))
    if b != 1:
        out = out | (last_h & (k == (3 if b == 0 else 2)))
    return onehot((n == source) & jnp.logical_not(out))


def add_taps(total, taps, x, k1):
    for first, (a, b, c) in enumerate(taps):
        i = (a * 3 + b) * 3 + c
        y = dot(x(b, c)[a : a + T].reshape(T * 64, C), k1[i * C : (i + 1) * C])
        if first == 0 and total[1] is None:
            total[0][...] = y
        elif first == 0:
            total[0][...] = total[1][...] + y
        else:
            total[0][...] += y


def own_kernel(
    at_ref, own_ref, one_ref, two_ref, three_ref, after_ref, k1, kd_ref, g_ref, xb, pre, kdt, kd, sems
):
    copies = fetch(kd_ref, kd, sems)
    for back, ref in enumerate((own_ref, one_ref, two_ref, three_ref)):
        g_ref[lax.rem(at_ref[0] + TA - back, TA)] = ref[...]
    pick = window_pick(at_ref, 0)[:, :64]
    for c in range(3):
        xb[c, 0:2] = jnp.zeros((2, 64, C), BF16)
    for t in range(T):
        s, low = t // F, 2 * W * (t % F)
        rows = [g_ref[s, low : low + 2 * W], g_ref[s, HEAD + low : HEAD + low + 2 * W]]
        built = dot(pick, jnp.concatenate(rows, axis=0)).astype(BF16)
        for c in range(3):
            xb[c, t + 2] = built[c * 64 : (c + 1) * 64]
    add_taps((pre, None), [x for x in TAPS if x[1] == 0], lambda b, c: xb.at[c], k1)
    turn(copies, kd, kdt)


def early_kernel(at_ref, g_ref, h_ref, k1, pre_ref, xb, pre, edge_ref):
    picks = [window_pick(at_ref, b) for b in range(3)]
    for b in range(3):
        edge_ref[b] = picks[b][64:, 96:]
    own = jnp.concatenate([picks[1][:, :96], picks[2][:, :96]], axis=0)
    for i in range(6):
        xb[i, 0:2] = jnp.zeros((2, 64, C), BF16)
    for t in range(T):
        built = dot(own, jnp.concatenate(frame_rows(g_ref, h_ref, t), axis=0)).astype(BF16)
        for i in range(6):
            xb[i, t + 2] = built[i * 64 : (i + 1) * 64]
    taps = [x for x in TAPS if x[1] != 0]
    add_taps((pre, pre_ref), taps, lambda b, c: xb.at[b * 3 + c - 3], k1)


SPILL = 48


def clip_pick(at_ref, b, c, rows, width, first):
    m, n = iota((rows, 64), 0), iota((rows, 64), 1)
    h, v = div(m, width), first + mod(m, width)
    k, col = div(n, W), column(mod(n, W))
    hit = (h == k + b) & (v == col + c) & (v < W + 2)
    if b != 1:
        hit = hit & jnp.logical_not((at_ref[1] == HA - 1) & (k == (3 if b == 0 else 2)))
    if c != 1:
        hit = hit & jnp.logical_not((at_ref[2] == WA - 1) & (col == (15 if c == 0 else 14)))
    return onehot(hit)


def middle_kernel(
    at_ref, g_ref, h_ref, w_ref, k1, k1t, kdt, pre_ref,
    gp, act, cu, spill_ref, pre, act32, fix, yb,
):
    ta, last_h, last_w = at_ref[0], at_ref[1] == HA - 1, at_ref[2] == WA - 1
    cot = 2 * F * W

    edges = w_ref[...].reshape(T * 16, C)
    m, n = iota((64, T * 16), 0), iota((64, T * 16), 1)
    t, k, e = div(m, 8), mod(div(m, 2), 4), mod(m, 2)
    total = None
    for i, (a, b, c) in enumerate(TAPS):
        if c == 0:
            continue
        hit = (n == (t - 2 + a) * 16 + (k + b) * 2 + e + (c - 2)) & (e + c >= 2)
        if b != 1:
            hit = hit & jnp.logical_not(last_h & (k == (3 if b == 0 else 2)))
        if c == 2:
            hit = hit & jnp.logical_not(last_w & (e == 0))
        y = dot(dot(onehot(hit), edges).astype(BF16), k1[i * C : (i + 1) * C])
        total = y if total is None else total + y
    fix[...] = total

    m, n = iota((144, 48), 0), iota((144, 48), 1)
    (b, c), place = third(div(m, 16)), mod(m, 16)
    kk, mm = div(place, 8), mod(place, 8)
    r, q = kk + jnp.where(b < 2, 1, 0), mm + jnp.where(c < 2, 1, 0)
    source = jnp.where(q == 8, 44 + r, r * 8 + q)
    out_h = last_h & (b == 0) & (kk == 1)
    out_w = last_w & (c == 0) & (mm == 7)
    pick = onehot((n == source) & jnp.logical_not(out_h | out_w))
    for i in range(9):
        cu[i, TA] = jnp.zeros((16, C), BF16)
    for j in range(TA):
        rows = jnp.concatenate(
            [g_ref[j, cot : cot + 16], h_ref[j, cot : cot + 16], w_ref[2 * j]], axis=0
        )
        built = dot(pick, rows).astype(BF16)
        for i in range(9):
            cu[i, j] = built[i * 16 : (i + 1) * 16]

    last = iota((8, C), 0) == 7
    for te in range(2):
        for ke in range(2):
            for ce in range(2):
                total = None
                for i, (a, b, c) in enumerate(TAPS):
                    if (a == 1, b == 1, c == 1) != (te == 1, ke == 1, ce == 1):
                        continue
                    ja = 1 if a < 2 else 0
                    y = dot(cu[b * 3 + c, ja : ja + 4].reshape(64, C), kdt[i * C : (i + 1) * C])
                    total = y if total is None else total + y
                for j in range(4):
                    for kk in range(2):
                        t, k = 2 * j + te, 2 * kk + ke
                        spot = t * 64 + k * W + ce * 8
                        late = (t * 4 + k) * 2 + ce
                        x = pre_ref[spot : spot + 8] + jnp.where(last, fix[late : late + 1], 0.0)
                        s = 1.0 / (1.0 + jnp.exp(-x))
                        at = (j * 2 + kk) * 8
                        g = total[at : at + 8]
                        act32[te * 4 + ke * 2 + ce, at : at + 8] = x * s
                        pre[spot : spot + 8] = g * s * (1.0 + x * (1.0 - s))
    gp[0:2] = jnp.zeros((2, 64, C), BF16)
    gp[2 : T + 2] = pre[...].astype(BF16).reshape(T, 64, C)
    gp[T + 2 : T + 4] = jnp.zeros((2, 64, C), BF16)
    act[...] = act32[...].astype(BF16)

    later = gp[pl.ds(2 + F * ta, F + 2)]
    pick = jnp.concatenate(
        [clip_pick(at_ref, b, c, SPILL, 8, W) for b in range(3) for c in (1, 2)], axis=0
    )
    for t in range(F + 2):
        built = dot(pick, later[t]).astype(BF16)
        for i in range(6):
            yb[i, t] = built[i * SPILL : (i + 1) * SPILL]
    total = None
    for i, (a, b, c) in enumerate(TAPS):
        if c == 0:
            continue
        x = yb[b * 2 + c - 1, 2 - a : 2 - a + F].reshape(F * SPILL, C)
        y = dot(x, k1t[i * C : (i + 1) * C])
        total = y if total is None else total + y
    spill_ref[...] = total.reshape(F, SPILL, C)


def main_kernel(
    at_ref, w_ref, xa_ref, xb_ref, edge_ref, gp, act, cu, mine_ref, other_ref, xc, tt
):
    ta, core = at_ref[0], lax.rem(at_ref[1], 2)

    share = onehot(iota((SHARE, C), 1) == iota((SHARE, C), 0) + ta * SHARE)
    left = jnp.concatenate(
        [
            dot_t(share, gp[2 - a : 2 - a + T + 2].reshape((T + 2) * 64, C)).astype(BF16)
            for a in range(3)
        ],
        axis=0,
    )
    late = edge_ref[...].reshape(6 * 64, 16)
    windows = [xa_ref.at[i] if i < 3 else xb_ref.at[i - 3] for i in range(9)]
    for i in range(6):
        xc[i, 0:2] = jnp.zeros((2, 64, C), BF16)
    for t in range(T):
        built = dot(late, w_ref[t]).astype(BF16)
        for i in range(6):
            base = windows[i // 2 * 3 + i % 2 + 1]
            xc[i, t + 2] = base[t + 2] + built[i * 64 : (i + 1) * 64]
    upper, lower = {}, {}
    for bc in range(9):
        x = windows[bc] if bc % 3 == 0 else xc.at[bc // 3 * 2 + bc % 3 - 1]
        y = dot(left, x[...].reshape((T + 2) * 64, C))
        for a in range(3):
            upper[a * 9 + bc] = y[a * SHARE : (a + 1) * SHARE]
    cots = {}
    for bc in range(9):
        for ja in range(2):
            cots[bc, ja] = dot_t(share, cu[bc, ja : ja + 4].reshape(64, C)).astype(BF16)
    for kind in range(8):
        taps = [
            (i, cots[b * 3 + c, 1 if a < 2 else 0])
            for i, (a, b, c) in enumerate(TAPS)
            if (a == 1) * 4 + (b == 1) * 2 + (c == 1) == kind
        ]
        y = dot(jnp.concatenate([x for _, x in taps], axis=0), act[kind])
        for place, (i, _) in enumerate(taps):
            lower[i] = y[place * SHARE : (place + 1) * SHARE]
    for i in range(27):
        tt[i * C : (i + 1) * C] = jnp.concatenate([upper[i], lower[i]], axis=0).T
    tt[27 * C :] = jnp.zeros((8, 2 * SHARE), F32)

    for x in range(HA // 2):
        for w in range(WA):
            pair = []
            for cc in range(2):
                first = ((x * 2 + cc) * WA + w) * PART
                y = tt[first : first + SLOT]
                pair.append(y)
            spot = (x * WA + w) * SLOT
            mine_ref[spot : spot + SLOT] = jnp.where(core == 0, pair[0], pair[1]).astype(BF16)
            other_ref[spot : spot + SLOT] = jnp.where(core == 0, pair[1], pair[0]).astype(BF16)


WIDE = 96


def clip_kernel(at_ref, gp, k1t, own_ref, past_ref, yb, acc):
    later = gp[pl.ds(2 + F * at_ref[0], F + 2)]
    pick = jnp.concatenate([clip_pick(at_ref, i // 3, i % 3, WIDE, W, 0) for i in range(9)], axis=0)
    for t in range(F + 2):
        built = dot(pick, later[t]).astype(BF16)
        for i in range(9):
            yb[i, t] = built[i * WIDE : (i + 1) * WIDE]
    for i, (a, b, c) in enumerate(TAPS):
        y = dot(yb[b * 3 + c, 2 - a : 2 - a + F].reshape(F * WIDE, C), k1t[i * C : (i + 1) * C])
        if i == 0:
            acc[...] = y
        else:
            acc[...] += y
    for f in range(F):
        own_ref[f] = acc[f * WIDE : f * WIDE + R * W]
        past_ref[f] = acc[f * WIDE + R * W : (f + 1) * WIDE]


def seam_kernel(past_ref, spill_ref, out_ref):
    for f in range(F):
        for h in range(2):
            at, spot = h * W, (R + h) * 8
            out_ref[f, at : at + 8] = past_ref[f, at : at + 8] + spill_ref[f, spot : spot + 8]
            out_ref[f, at + 8 : at + W] = past_ref[f, at + 8 : at + W]


STAGES = 4


def join_kernel(mine_ref, other_ref, after_ref, out_ref, joined, sems):
    rows = PEERS * SLOT // STAGES
    copies = []
    for i in range(STAGES):
        part = pl.ds(i * rows, rows)
        joined[part] = mine_ref[part] + other_ref[part]
        copies.append(pltpu.make_async_copy(joined.at[part], out_ref.at[part], sems.at[i]))
        copies[-1].start()
    for copy in copies:
        copy.wait()


def finish_kernel(parts_ref, own_ref, spill_ref, past_ref, clip_ref, conv_ref, down_ref):
    for f in range(F):
        for h in range(R):
            at = h * W
            low = own_ref[f, at : at + 8] + spill_ref[f, h * 8 : h * 8 + 8]
            x = jnp.concatenate([low, own_ref[f, at + 8 : at + W]], axis=0)
            if h < 2:
                x += past_ref[f, at : at + W]
            clip_ref[f, at : at + W] = x.astype(BF16)
    total = parts_ref[0].astype(F32)
    for i in range(1, PEERS):
        total += parts_ref[i].astype(F32)
    total = jnp.concatenate([total, jnp.zeros((128 - SLOT, 2 * SHARE), F32)], axis=0).T
    conv_ref[...] = total[:SHARE, :PART]
    down_ref[...] = total[SHARE:, :PART]


def whole():
    return pl.BlockSpec(memory_space=pltpu.VMEM)


def call(kernel, outs, specs, scratch, flops, name, out=None):
    return pl.pallas_call(
        kernel,
        out_shape=outs,
        in_specs=specs,
        out_specs=jax.tree.map(lambda _: out or whole(), outs),
        scratch_shapes=scratch,
        compiler_params=pltpu.CompilerParams(vmem_limit_bytes=VMEM_BYTES),
        cost_estimate=pl.CostEstimate(flops=flops, bytes_accessed=8_000_000, transcendentals=0),
        name=name,
    )


def shape(dims, dtype=BF16):
    return jax.ShapeDtypeStruct(dims, dtype)


def on_chip(dims, dtype=BF16):
    return pltpu.VMEM(dims, dtype)


def in_hbm(x):
    return pltpu.with_memory_space_constraint(x, pltpu.HBM)


def in_vmem(x):
    return pltpu.with_memory_space_constraint(x, pltpu.VMEM)


def shift(x, axis, by):
    count = lax.axis_size(axis)
    return lax.ppermute(x, axis, [(i, (i + by) % count) for i in range(count)])


def local(clip, conv_weight, down_weight, out_cotangent):
    smem, anywhere = pl.BlockSpec(memory_space=pltpu.SMEM), pl.BlockSpec(memory_space=pl.ANY)
    at = jnp.stack([lax.axis_index(a) for a in ("ta", "ha", "wa")]).astype(jnp.int32)
    dma = pltpu.SemaphoreType.DMA
    packed = call(
        pack_kernel, shape((BLOCK, C)), [anywhere] * 2, [dma((9,))], 10**5, "pack"
    )(in_hbm(clip), in_hbm(out_cotangent.reshape(-1, C)))
    around = [shift(packed, "ta", by) for by in (1, 2, 3)]
    weight = on_chip((27 * C, C))
    k1, k1t = call(
        load_kernel,
        [weight] * 2,
        [smem] + [anywhere] * 2,
        [dma((9,))],
        2 * 10**9,
        "load",
    )(at, packed, in_hbm(conv_weight))
    k1, k1t = in_vmem(k1), in_vmem(k1t)
    head = call(
        head_kernel,
        shape((TA, HEAD, C)),
        [smem] + [whole()] * 4 + [anywhere],
        [],
        10**5,
        "head",
    )(at, packed, *around, k1t)
    h = shift(head, "ha", -1)
    g, xa, pre, kdt = call(
        own_kernel,
        [shape((TA, BLOCK, C)), on_chip((3, T + 2, 64, C)), on_chip((T * 64, C), F32), weight],
        [smem] + [whole()] * 4 + [anywhere, whole(), anywhere],
        [pltpu.VMEM((27 * C, C), BF16), dma((9,))],
        3 * 10**9,
        "own",
    )(at, packed, *around, head, k1, in_hbm(down_weight))
    xa, pre, kdt = in_vmem(xa), in_vmem(pre), in_vmem(kdt)
    w = call(edge_kernel, shape((T, 16, C)), [whole()] * 2, [], 10**7, "edge")(g, h)
    w = shift(w, "wa", -1)
    xb, pre, edge = call(
        early_kernel,
        [on_chip((6, T + 2, 64, C)), on_chip((T * 64, C), F32), on_chip((3, 128, 16))],
        [smem] + [whole()] * 4,
        [],
        3 * 10**9,
        "early",
    )(at, g, h, k1, pre)
    xb, pre, edge = in_vmem(xb), in_vmem(pre), in_vmem(edge)
    gp, act, cu, spill = call(
        middle_kernel,
        [
            on_chip((T + 4, 64, C)),
            on_chip((8, 64, C)),
            on_chip((9, TA + 1, 16, C)),
            shape((F, SPILL, C), F32),
        ],
        [smem] + [whole()] * 7,
        [
            pltpu.VMEM((T * 64, C), F32),
            pltpu.VMEM((8, 64, C), F32),
            pltpu.VMEM((64, C), F32),
            pltpu.VMEM((6, F + 2, SPILL, C), BF16),
        ],
        3 * 10**9,
        "middle",
    )(at, g, h, w, k1, k1t, kdt, pre)
    gp, act, cu = in_vmem(gp), in_vmem(act), in_vmem(cu)
    spill = shift(spill, "wa", 1)
    mine, other = call(
        main_kernel,
        [shape((PEERS * SLOT, 2 * SHARE)), shape((PEERS * SLOT, 2 * SHARE))],
        [smem] + [whole()] * 7,
        [pltpu.VMEM((6, T + 2, 64, C), BF16), pltpu.VMEM((27 * C + 8, 2 * SHARE), F32)],
        5 * 10**9,
        "main",
    )(at, w, xa, xb, edge, gp, act, cu)
    other = lax.ppermute(other, "ha", [(i, i ^ 1) for i in range(HA)])
    own, past = call(
        clip_kernel,
        [shape((F, R * W, C), F32), shape((F, 2 * W, C), F32)],
        [smem] + [whole()] * 2,
        [pltpu.VMEM((9, F + 2, WIDE, C), BF16), pltpu.VMEM((F * WIDE, C), F32)],
        10**9,
        "clip",
    )(at, gp, k1t)
    pair = call(
        join_kernel,
        shape((PEERS * SLOT, 2 * SHARE)),
        [whole(), whole(), anywhere],
        [pltpu.VMEM((PEERS * SLOT, 2 * SHARE), BF16), dma((STAGES,))],
        10**6,
        "join",
        anywhere,
    )(mine, other, own)
    pair, spill = lax.optimization_barrier((pair, spill))
    past = call(
        seam_kernel, shape((F, 2 * W, C), F32), [whole()] * 2, [], 10**5, "seam"
    )(past, spill)
    past = shift(past, "ha", 1)
    groups = [[i * WA + w for i in range(c, HA, 2) for w in range(WA)] for c in range(2)]
    parts = lax.all_to_all(pair, ("ha", "wa"), 0, 0, axis_index_groups=groups, tiled=True)
    grad_clip, grad_conv, grad_down = call(
        finish_kernel,
        [shape((F, R * W, C)), shape((SHARE, PART), F32), shape((SHARE, PART), F32)],
        [whole()] * 4,
        [],
        10**6,
        "finish",
    )(parts.reshape(PEERS, SLOT, 2 * SHARE), own, spill, past)
    grad_clip = grad_clip.reshape(F, R, W, C)
    return (grad_clip, grad_conv.T, grad_down.T)


def solution(mesh):
    return jax.shard_map(
        local,
        mesh=mesh,
        in_specs=(P("ta", "ha", "wa", None), P(), P(), P("ta", "ha", "wa", None)),
        out_specs=(P("ta", "ha", "wa", None), P(("ha", "wa"), "ta"), P(("ha", "wa"), "ta")),
        check_vma=False,
    )
```

```python
import jax
import jax.numpy as jnp
from jax import lax
from jax.experimental import pallas as pl
from jax.experimental.pallas import tpu as pltpu
from jax.sharding import PartitionSpec as P

F, R, W, C = 2, 4, 16, 256
TA, HA, WA = 4, 8, 8
T = TA * F
HEAD = 2 * F * W + (R // 2) * (W // 2)
BLOCK = F * R * W + (R // 2) * (W // 2)
SHARE = C // TA
PART = 27 * C // (HA * WA)
SLOT = 112
PEERS = HA * WA // 2
TAPS = [(a, b, c) for a in range(3) for b in range(3) for c in range(3)]
BF16, F32 = jnp.bfloat16, jnp.float32
VMEM_BYTES = 28 * 1024 * 1024


def iota(shape, dim):
    return lax.broadcasted_iota(jnp.int32, shape, dim)


def onehot(hit):
    return jnp.where(hit, 1.0, 0.0).astype(F32).astype(BF16)


def div(x, n):
    return lax.shift_right_logical(x, n.bit_length() - 1)


def mod(x, n):
    return lax.bitwise_and(x, n - 1)


def third(x):
    high = jnp.where(x >= 3, 1, 0) + jnp.where(x >= 6, 1, 0)
    return high, x - 3 * high


def dot(x, y):
    return jnp.dot(x, y, preferred_element_type=F32)


def dot_t(x, y):
    return lax.dot_general(x, y, (((1,), (1,)), ((), ())), preferred_element_type=F32)


def column(order):
    return jnp.where(order < W // 2, 2 * order, 2 * (order - W // 2) + 1)


def frame_rows(g_ref, h_ref, t):
    s, f = t // F, t % F
    low = 2 * W * f
    return [
        g_ref[s, low : low + 2 * W],
        g_ref[s, HEAD + low : HEAD + low + 2 * W],
        h_ref[s, low : low + 2 * W],
    ]


def edge_kernel(g_ref, h_ref, out_ref):
    cot = 2 * F * W
    m, n = iota((16, 128), 0), iota((16, 128), 1)
    source = jnp.where(m < 12, div(m, 2) * W + mod(m, 2), jnp.where(m < 14, 96 + (m - 12) * 8, 112))
    pick = onehot((n == source) & (m < 15))
    for t in range(T):
        s = t // F
        rows = frame_rows(g_ref, h_ref, t) + [g_ref[s, cot : cot + 16], h_ref[s, cot : cot + 16]]
        out_ref[t] = dot(pick, jnp.concatenate(rows, axis=0)).astype(BF16)


def pack_kernel(clip_ref, cot_ref, out_ref, sems):
    half = 2 * W
    copies = []
    for f in range(F):
        for part in range(2):
            spot = part * HEAD + f * half
            copies.append((clip_ref.at[2 * f + part], out_ref.at[pl.ds(spot, half)]))
    copies.append((cot_ref, out_ref.at[pl.ds(2 * F * W, 16)]))
    copies = [pltpu.make_async_copy(x, y, sems.at[i]) for i, (x, y) in enumerate(copies)]
    for copy in copies:
        copy.start()
    for copy in copies:
        copy.wait()


def head_kernel(own_ref, one_ref, two_ref, three_ref, after_ref, head_ref):
    for back, ref in enumerate((own_ref, one_ref, two_ref, three_ref)):
        head_ref[lax.rem(lax.axis_index("ta") + TA - back, TA)] = ref[:HEAD]


def fetch(source, target, sems):
    step = 3 * C
    parts = [pl.ds(i * step, step) for i in range(9)]
    copies = [
        pltpu.make_async_copy(source.at[part], target.at[part], sems.at[i])
        for i, part in enumerate(parts)
    ]
    for copy in copies:
        copy.start()
    return copies


def turn(copies, plain, turned):
    for i in range(27):
        if i % 3 == 0:
            copies[i // 3].wait()
        turned[i * C : (i + 1) * C] = plain[i * C : (i + 1) * C].T


def load_kernel(after_ref, k1_ref, kd_ref, k1, k1t, kdt, kd, sems1, semsd):
    first, second = fetch(k1_ref, k1, sems1), fetch(kd_ref, kd, semsd)
    turn(first, k1, k1t)
    turn(second, kd, kdt)


def window_pick(b):
    last_h, last_w = lax.axis_index("ha") == HA - 1, lax.axis_index("wa") == WA - 1
    m, n = iota((192, 112), 0), iota((192, 112), 1)
    c, place = div(m, 64), mod(m, 64)
    k, col = div(place, W), column(mod(place, W))
    row, v = k + b, col + c
    source = jnp.where(v < W, row * W + v, 96 + row * 2 + v - W)
    out = last_w & (((c == 0) & (col == 15)) | ((c == 2) & (col == 14)))
    if b != 1:
        out = out | (last_h & (k == (3 if b == 0 else 2)))
    return onehot((n == source) & jnp.logical_not(out))


def add_taps(total, taps, x, k1):
    for first, (a, b, c) in enumerate(taps):
        i = (a * 3 + b) * 3 + c
        y = dot(x(b, c)[a : a + T].reshape(T * 64, C), k1[i * C : (i + 1) * C])
        if first == 0 and total[1] is None:
            total[0][...] = y
        elif first == 0:
            total[0][...] = total[1][...] + y
        else:
            total[0][...] += y


def own_kernel(
    own_ref, one_ref, two_ref, three_ref, after_ref, k1, g_ref, xb, pre
):
    for back, ref in enumerate((own_ref, one_ref, two_ref, three_ref)):
        g_ref[lax.rem(lax.axis_index("ta") + TA - back, TA)] = ref[...]
    pick = window_pick(0)[:, :64]
    for c in range(3):
        xb[c, 0:2] = jnp.zeros((2, 64, C), BF16)
    for t in range(T):
        s, low = t // F, 2 * W * (t % F)
        rows = [g_ref[s, low : low + 2 * W], g_ref[s, HEAD + low : HEAD + low + 2 * W]]
        built = dot(pick, jnp.concatenate(rows, axis=0)).astype(BF16)
        for c in range(3):
            xb[c, t + 2] = built[c * 64 : (c + 1) * 64]
    add_taps((pre, None), [x for x in TAPS if x[1] == 0], lambda b, c: xb.at[c], k1)


def early_kernel(g_ref, h_ref, k1, pre_ref, xb, pre, edge_ref):
    picks = [window_pick(b) for b in range(3)]
    for b in range(3):
        edge_ref[b] = picks[b][64:, 96:]
    own = jnp.concatenate([picks[1][:, :96], picks[2][:, :96]], axis=0)
    for i in range(6):
        xb[i, 0:2] = jnp.zeros((2, 64, C), BF16)
    for t in range(T):
        built = dot(own, jnp.concatenate(frame_rows(g_ref, h_ref, t), axis=0)).astype(BF16)
        for i in range(6):
            xb[i, t + 2] = built[i * 64 : (i + 1) * 64]
    taps = [x for x in TAPS if x[1] != 0]
    add_taps((pre, pre_ref), taps, lambda b, c: xb.at[b * 3 + c - 3], k1)


SPILL = 16


def clip_pick(b, c, rows, width, first):
    m, n = iota((rows, 64), 0), iota((rows, 64), 1)
    h, v = div(m, width), first + mod(m, width)
    k, col = div(n, W), column(mod(n, W))
    hit = (h == k + b) & (v == col + c) & (v < W + 2)
    if b != 1:
        hit = hit & jnp.logical_not((lax.axis_index("ha") == HA - 1) & (k == (3 if b == 0 else 2)))
    if c != 1:
        hit = hit & jnp.logical_not((lax.axis_index("wa") == WA - 1) & (col == (15 if c == 0 else 14)))
    return onehot(hit)


def middle_kernel(
    g_ref, h_ref, w_ref, k1, kdt, pre_ref, gp, act, cu, pre, act32, fix
):
    ta, last_h, last_w = lax.axis_index("ta"), lax.axis_index("ha") == HA - 1, lax.axis_index("wa") == WA - 1
    cot = 2 * F * W

    edges = w_ref[...].reshape(T * 16, C)
    m, n = iota((64, T * 16), 0), iota((64, T * 16), 1)
    t, k, e = div(m, 8), mod(div(m, 2), 4), mod(m, 2)
    total = None
    for i, (a, b, c) in enumerate(TAPS):
        if c == 0:
            continue
        hit = (n == (t - 2 + a) * 16 + (k + b) * 2 + e + (c - 2)) & (e + c >= 2)
        if b != 1:
            hit = hit & jnp.logical_not(last_h & (k == (3 if b == 0 else 2)))
        if c == 2:
            hit = hit & jnp.logical_not(last_w & (e == 0))
        y = dot(dot(onehot(hit), edges).astype(BF16), k1[i * C : (i + 1) * C])
        total = y if total is None else total + y
    fix[...] = total

    m, n = iota((144, 48), 0), iota((144, 48), 1)
    (b, c), place = third(div(m, 16)), mod(m, 16)
    kk, mm = div(place, 8), mod(place, 8)
    r, q = kk + jnp.where(b < 2, 1, 0), mm + jnp.where(c < 2, 1, 0)
    source = jnp.where(q == 8, 44 + r, r * 8 + q)
    out_h = last_h & (b == 0) & (kk == 1)
    out_w = last_w & (c == 0) & (mm == 7)
    pick = onehot((n == source) & jnp.logical_not(out_h | out_w))
    for i in range(9):
        cu[i, TA] = jnp.zeros((16, C), BF16)
    for j in range(TA):
        rows = jnp.concatenate(
            [g_ref[j, cot : cot + 16], h_ref[j, cot : cot + 16], w_ref[2 * j]], axis=0
        )
        built = dot(pick, rows).astype(BF16)
        for i in range(9):
            cu[i, j] = built[i * 16 : (i + 1) * 16]

    last = iota((8, C), 0) == 7
    for te in range(2):
        for ke in range(2):
            for ce in range(2):
                total = None
                for i, (a, b, c) in enumerate(TAPS):
                    if (a == 1, b == 1, c == 1) != (te == 1, ke == 1, ce == 1):
                        continue
                    ja = 1 if a < 2 else 0
                    y = dot(cu[b * 3 + c, ja : ja + 4].reshape(64, C), kdt[i * C : (i + 1) * C])
                    total = y if total is None else total + y
                for j in range(4):
                    for kk in range(2):
                        t, k = 2 * j + te, 2 * kk + ke
                        spot = t * 64 + k * W + ce * 8
                        late = (t * 4 + k) * 2 + ce
                        x = pre_ref[spot : spot + 8] + jnp.where(last, fix[late : late + 1], 0.0)
                        s = 1.0 / (1.0 + jnp.exp(-x))
                        at = (j * 2 + kk) * 8
                        g = total[at : at + 8]
                        act32[te * 4 + ke * 2 + ce, at : at + 8] = x * s
                        pre[spot : spot + 8] = g * s * (1.0 + x * (1.0 - s))
    gp[0:2] = jnp.zeros((2, 64, C), BF16)
    gp[2 : T + 2] = pre[...].astype(BF16).reshape(T, 64, C)
    gp[T + 2 : T + 4] = jnp.zeros((2, 64, C), BF16)
    act[...] = act32[...].astype(BF16)


def main_kernel(
    w_ref, xa_ref, xb_ref, edge_ref, gp, act, cu, mine_ref, other_ref, xc, tt
):
    ta, core = lax.axis_index("ta"), lax.rem(lax.axis_index("ha"), 2)

    share = onehot(iota((SHARE, C), 1) == iota((SHARE, C), 0) + ta * SHARE)
    turned = dot_t(share, gp[...].reshape((T + 4) * 64, C))
    left = jnp.concatenate(
        [turned[:, (2 - a) * 64 : (2 - a + T + 2) * 64] for a in range(3)], axis=0
    ).astype(BF16)
    late = edge_ref[...].reshape(6 * 64, 16)
    windows = [xa_ref.at[i] if i < 3 else xb_ref.at[i - 3] for i in range(9)]
    for i in range(6):
        xc[i, 0:2] = jnp.zeros((2, 64, C), BF16)
    for t in range(T):
        built = dot(late, w_ref[t]).astype(BF16)
        for i in range(6):
            base = windows[i // 2 * 3 + i % 2 + 1]
            xc[i, t + 2] = base[t + 2] + built[i * 64 : (i + 1) * 64]
    upper, lower = {}, {}
    for bc in range(9):
        x = windows[bc] if bc % 3 == 0 else xc.at[bc // 3 * 2 + bc % 3 - 1]
        y = dot(left, x[...].reshape((T + 2) * 64, C))
        for a in range(3):
            upper[a * 9 + bc] = y[a * SHARE : (a + 1) * SHARE]
    cots = {}
    for bc in range(9):
        for ja in range(2):
            cots[bc, ja] = dot_t(share, cu[bc, ja : ja + 4].reshape(64, C)).astype(BF16)
    for kind in range(8):
        taps = [
            (i, cots[b * 3 + c, 1 if a < 2 else 0])
            for i, (a, b, c) in enumerate(TAPS)
            if (a == 1) * 4 + (b == 1) * 2 + (c == 1) == kind
        ]
        y = dot(jnp.concatenate([x for _, x in taps], axis=0), act[kind])
        for place, (i, _) in enumerate(taps):
            lower[i] = y[place * SHARE : (place + 1) * SHARE]
    for i in range(27):
        tt[i * C : (i + 1) * C] = jnp.concatenate([upper[i], lower[i]], axis=0).T
    tt[27 * C :] = jnp.zeros((8, 2 * SHARE), F32)

    for x in range(HA // 2):
        for w in range(WA):
            pair = []
            for cc in range(2):
                first = ((x * 2 + cc) * WA + w) * PART
                y = tt[first : first + SLOT]
                pair.append(y)
            spot = (x * WA + w) * SLOT
            mine_ref[spot : spot + SLOT] = jnp.where(core == 0, pair[0], pair[1]).astype(BF16)
            other_ref[spot : spot + SLOT] = jnp.where(core == 0, pair[1], pair[0]).astype(BF16)


MAIN = (R + 2) * W
WIDE = MAIN + SPILL


def clip_kernel(gp, k1t, own_ref, past_ref, spill_ref, yb, acc):
    later = gp[pl.ds(2 + F * lax.axis_index("ta"), F + 2)]
    for i in range(9):
        b, c = i // 3, i % 3
        pick = jnp.concatenate([clip_pick(b, c, MAIN, W, 0), clip_pick(b, c, SPILL, 2, W)], axis=0)
        for t in range(F + 2):
            yb[i, t] = dot(pick, later[t]).astype(BF16)
    for i, (a, b, c) in enumerate(TAPS):
        x = yb[b * 3 + c, 2 - a : 2 - a + F].reshape(F * WIDE, C)
        y = dot(x, k1t[i * C : (i + 1) * C])
        if i == 0:
            acc[...] = y
        else:
            acc[...] += y
    for f in range(F):
        own_ref[f] = acc[f * WIDE : f * WIDE + R * W]
        past_ref[f] = acc[f * WIDE + R * W : f * WIDE + MAIN]
        spill_ref[f] = acc[f * WIDE + MAIN : (f + 1) * WIDE]


def spilled(spill_ref, f, h):
    place = iota((8, C), 0)
    first, second = spill_ref[f, 2 * h : 2 * h + 1], spill_ref[f, 2 * h + 1 : 2 * h + 2]
    return jnp.where(place == 0, first, jnp.where(place == 1, second, 0.0))


STAGES = 4


def join_kernel(mine_ref, other_ref, after_ref, out_ref, joined, sems):
    rows = PEERS * SLOT // STAGES
    copies = []
    for i in range(STAGES):
        part = pl.ds(i * rows, rows)
        joined[part] = mine_ref[part] + other_ref[part]
        copies.append(pltpu.make_async_copy(joined.at[part], out_ref.at[part], sems.at[i]))
        copies[-1].start()
    for copy in copies:
        copy.wait()


def finish_kernel(
    parts_ref, own_ref, spill_ref, past_ref, corner_ref, clip_ref, conv_ref, down_ref
):
    for f in range(F):
        for h in range(R):
            at = h * W
            low = own_ref[f, at : at + 8] + spilled(spill_ref, f, h)
            high = own_ref[f, at + 8 : at + W]
            if h < 2:
                low += past_ref[f, at : at + 8] + spilled(corner_ref, f, R + h)
                high += past_ref[f, at + 8 : at + W]
            clip_ref[f, at : at + W] = jnp.concatenate([low, high], axis=0).astype(BF16)
    total = parts_ref[0].astype(F32)
    for i in range(1, PEERS):
        total += parts_ref[i].astype(F32)
    total = jnp.concatenate([total, jnp.zeros((128 - SLOT, 2 * SHARE), F32)], axis=0).T
    conv_ref[...] = total[:SHARE, :PART]
    down_ref[...] = total[SHARE:, :PART]


def whole():
    return pl.BlockSpec(memory_space=pltpu.VMEM)


def call(kernel, outs, specs, scratch, flops, name, out=None):
    return pl.pallas_call(
        kernel,
        out_shape=outs,
        in_specs=specs,
        out_specs=jax.tree.map(lambda _: out or whole(), outs),
        scratch_shapes=scratch,
        compiler_params=pltpu.CompilerParams(vmem_limit_bytes=VMEM_BYTES),
        cost_estimate=pl.CostEstimate(flops=flops, bytes_accessed=10_000, transcendentals=0),
        name=name,
    )


def shape(dims, dtype=BF16):
    return jax.ShapeDtypeStruct(dims, dtype)


def on_chip(dims, dtype=BF16):
    return pltpu.VMEM(dims, dtype)


def in_hbm(x):
    return pltpu.with_memory_space_constraint(x, pltpu.HBM)


def in_vmem(x):
    return pltpu.with_memory_space_constraint(x, pltpu.VMEM)


def shift(x, axis, by):
    count = lax.axis_size(axis)
    return lax.ppermute(x, axis, [(i, (i + by) % count) for i in range(count)])


def local(clip, conv_weight, down_weight, out_cotangent):
    anywhere = pl.BlockSpec(memory_space=pl.ANY)
    dma = pltpu.SemaphoreType.DMA
    packed = call(
        pack_kernel, shape((BLOCK, C)), [anywhere] * 2, [dma((5,))], 10**5, "pack"
    )(in_hbm(clip.reshape(2 * F, 2 * W, C)), in_hbm(out_cotangent.reshape(-1, C)))
    around = [shift(packed, "ta", by) for by in (1, 2, 3)]
    weight = on_chip((27 * C, C))
    k1, k1t, kdt = call(
        load_kernel,
        [weight] * 3,
        [anywhere] * 3,
        [pltpu.VMEM((27 * C, C), BF16), dma((9,)), dma((9,))],
        4 * 10**9,
        "load",
    )(packed, in_hbm(conv_weight), in_hbm(down_weight))
    k1, k1t, kdt = in_vmem(k1), in_vmem(k1t), in_vmem(kdt)
    head = call(
        head_kernel,
        shape((TA, HEAD, C)),
        [whole()] * 4 + [anywhere],
        [],
        10**5,
        "head",
    )(packed, *around, k1t)
    h = shift(head, "ha", -1)
    g, xa, pre = call(
        own_kernel,
        [shape((TA, BLOCK, C)), on_chip((3, T + 2, 64, C)), on_chip((T * 64, C), F32)],
        [whole()] * 4 + [anywhere, whole()],
        [],
        3 * 10**9,
        "own",
    )(packed, *around, head, k1)
    xa, pre = in_vmem(xa), in_vmem(pre)
    w = call(edge_kernel, shape((T, 16, C)), [whole()] * 2, [], 10**7, "edge")(g, h)
    w = shift(w, "wa", -1)
    xb, pre, edge = call(
        early_kernel,
        [on_chip((6, T + 2, 64, C)), on_chip((T * 64, C), F32), on_chip((3, 128, 16))],
        [whole()] * 4,
        [],
        3 * 10**9,
        "early",
    )(g, h, k1, pre)
    xb, pre, edge = in_vmem(xb), in_vmem(pre), in_vmem(edge)
    gp, act, cu = call(
        middle_kernel,
        [
            on_chip((T + 4, 64, C)),
            on_chip((8, 64, C)),
            on_chip((9, TA + 1, 16, C)),
        ],
        [whole()] * 6,
        [
            pltpu.VMEM((T * 64, C), F32),
            pltpu.VMEM((8, 64, C), F32),
            pltpu.VMEM((64, C), F32),
        ],
        3 * 10**9,
        "middle",
    )(g, h, w, k1, kdt, pre)
    gp, act, cu = in_vmem(gp), in_vmem(act), in_vmem(cu)
    mine, other = call(
        main_kernel,
        [shape((PEERS * SLOT, 2 * SHARE)), shape((PEERS * SLOT, 2 * SHARE))],
        [whole()] * 7,
        [pltpu.VMEM((6, T + 2, 64, C), BF16), pltpu.VMEM((27 * C + 8, 2 * SHARE), F32)],
        5 * 10**9,
        "main",
    )(w, xa, xb, edge, gp, act, cu)
    other = lax.ppermute(other, "ha", [(i, i ^ 1) for i in range(HA)])
    own, past, spill = call(
        clip_kernel,
        [shape((F, R * W, C), F32), shape((F, 2 * W, C), F32), shape((F, SPILL, C), F32)],
        [whole()] * 2,
        [pltpu.VMEM((9, F + 2, WIDE, C), BF16), pltpu.VMEM((F * WIDE, C), F32)],
        10**9,
        "clip",
    )(gp, k1t)
    pair = call(
        join_kernel,
        shape((PEERS * SLOT, 2 * SHARE)),
        [whole(), whole(), anywhere],
        [pltpu.VMEM((PEERS * SLOT, 2 * SHARE), BF16), dma((STAGES,))],
        10**6,
        "join",
        anywhere,
    )(mine, other, own)
    pairs = [(i * WA + j, (i + 1) % HA * WA + (j + 1) % WA) for i in range(HA) for j in range(WA)]
    corner = lax.ppermute(spill, ("ha", "wa"), pairs)
    spill = shift(spill, "wa", 1)
    past = shift(past, "ha", 1)
    groups = [[i * WA + w for i in range(c, HA, 2) for w in range(WA)] for c in range(2)]
    parts = lax.all_to_all(pair, ("ha", "wa"), 0, 0, axis_index_groups=groups, tiled=True)
    grad_clip, grad_conv, grad_down = call(
        finish_kernel,
        [shape((F, R * W, C)), shape((SHARE, PART), F32), shape((SHARE, PART), F32)],
        [whole()] * 5,
        [],
        10**6,
        "finish",
    )(parts.reshape(PEERS, SLOT, 2 * SHARE), own, spill, past, corner)
    grad_clip = grad_clip.reshape(F, R, W, C)
    return (grad_clip, grad_conv.T, grad_down.T)


def solution(mesh):
    return jax.shard_map(
        local,
        mesh=mesh,
        in_specs=(P("ta", "ha", "wa", None), P(), P(), P("ta", "ha", "wa", None)),
        out_specs=(P("ta", "ha", "wa", None), P(("ha", "wa"), "ta"), P(("ha", "wa"), "ta")),
        check_vma=False,
    )
```

```python
import jax
import jax.numpy as jnp
from jax import lax
from jax.experimental import pallas as pl
from jax.experimental.pallas import tpu as pltpu
from jax.sharding import PartitionSpec as P

F, R, W, C = 2, 4, 16, 256
TA, HA, WA = 4, 8, 8
T = TA * F
HEAD = 2 * F * W + (R // 2) * (W // 2)
BLOCK = F * R * W + (R // 2) * (W // 2)
SHARE = C // TA
PART = 27 * C // (HA * WA)
SLOT = 112
PEERS = HA * WA // 2
TAPS = [(a, b, c) for a in range(3) for b in range(3) for c in range(3)]
BF16, F32 = jnp.bfloat16, jnp.float32
VMEM_BYTES = 28 * 1024 * 1024


def iota(shape, dim):
    return lax.broadcasted_iota(jnp.int32, shape, dim)


def onehot(hit):
    return jnp.where(hit, 1.0, 0.0).astype(F32).astype(BF16)


def div(x, n):
    return lax.shift_right_logical(x, n.bit_length() - 1)


def mod(x, n):
    return lax.bitwise_and(x, n - 1)


def third(x):
    high = jnp.where(x >= 3, 1, 0) + jnp.where(x >= 6, 1, 0)
    return high, x - 3 * high


def dot(x, y):
    return jnp.dot(x, y, preferred_element_type=F32)


def dot_t(x, y):
    return lax.dot_general(x, y, (((1,), (1,)), ((), ())), preferred_element_type=F32)


def column(order):
    return jnp.where(order < W // 2, 2 * order, 2 * (order - W // 2) + 1)


def frame_rows(g_ref, h_ref, t):
    s, f = t // F, t % F
    low = 2 * W * f
    return [
        g_ref[s, low : low + 2 * W],
        g_ref[s, HEAD + low : HEAD + low + 2 * W],
        h_ref[s, low : low + 2 * W],
    ]


def edge_kernel(g_ref, h_ref, out_ref):
    cot = 2 * F * W
    m, n = iota((16, 128), 0), iota((16, 128), 1)
    source = jnp.where(m < 12, div(m, 2) * W + mod(m, 2), jnp.where(m < 14, 96 + (m - 12) * 8, 112))
    pick = onehot((n == source) & (m < 15))
    for t in range(T):
        s = t // F
        rows = frame_rows(g_ref, h_ref, t) + [g_ref[s, cot : cot + 16], h_ref[s, cot : cot + 16]]
        out_ref[t] = dot(pick, jnp.concatenate(rows, axis=0)).astype(BF16)


def pack_kernel(clip_ref, cot_ref, out_ref, sems):
    half = 2 * W
    copies = []
    for f in range(F):
        for part in range(2):
            spot = part * HEAD + f * half
            copies.append((clip_ref.at[2 * f + part], out_ref.at[pl.ds(spot, half)]))
    copies.append((cot_ref, out_ref.at[pl.ds(2 * F * W, 16)]))
    copies = [pltpu.make_async_copy(x, y, sems.at[i]) for i, (x, y) in enumerate(copies)]
    for copy in copies:
        copy.start()
    for copy in copies:
        copy.wait()


def head_kernel(own_ref, one_ref, two_ref, three_ref, after_ref, head_ref):
    for back, ref in enumerate((own_ref, one_ref, two_ref, three_ref)):
        head_ref[lax.rem(lax.axis_index("ta") + TA - back, TA)] = ref[:HEAD]


def fetch(source, target, sems):
    step = 3 * C
    parts = [pl.ds(i * step, step) for i in range(9)]
    copies = [
        pltpu.make_async_copy(source.at[part], target.at[part], sems.at[i])
        for i, part in enumerate(parts)
    ]
    for copy in copies:
        copy.start()
    return copies


def turn(copies, plain, turned):
    for i in range(27):
        if i % 3 == 0:
            copies[i // 3].wait()
        turned[i * C : (i + 1) * C] = plain[i * C : (i + 1) * C].T


def load_kernel(after_ref, k1_ref, kd_ref, k1, k1t, kdt, kd, sems1, semsd):
    first, second = fetch(k1_ref, k1, sems1), fetch(kd_ref, kd, semsd)
    turn(first, k1, k1t)
    turn(second, kd, kdt)


def window_pick(b):
    last_h, last_w = lax.axis_index("ha") == HA - 1, lax.axis_index("wa") == WA - 1
    m, n = iota((192, 112), 0), iota((192, 112), 1)
    c, place = div(m, 64), mod(m, 64)
    k, col = div(place, W), column(mod(place, W))
    row, v = k + b, col + c
    source = jnp.where(v < W, row * W + v, 96 + row * 2 + v - W)
    out = last_w & (((c == 0) & (col == 15)) | ((c == 2) & (col == 14)))
    if b != 1:
        out = out | (last_h & (k == (3 if b == 0 else 2)))
    return onehot((n == source) & jnp.logical_not(out))


def add_taps(total, taps, x, k1):
    for first, (a, b, c) in enumerate(taps):
        i = (a * 3 + b) * 3 + c
        y = dot(x(b, c)[a : a + T].reshape(T * 64, C), k1[i * C : (i + 1) * C])
        if first == 0 and total[1] is None:
            total[0][...] = y
        elif first == 0:
            total[0][...] = total[1][...] + y
        else:
            total[0][...] += y


def own_kernel(
    own_ref, one_ref, two_ref, three_ref, after_ref, k1, g_ref, xb, pre
):
    for back, ref in enumerate((own_ref, one_ref, two_ref, three_ref)):
        g_ref[lax.rem(lax.axis_index("ta") + TA - back, TA)] = ref[...]
    pick = window_pick(0)[:, :64]
    for c in range(3):
        xb[c, 0:2] = jnp.zeros((2, 64, C), BF16)
    for t in range(T):
        s, low = t // F, 2 * W * (t % F)
        rows = [g_ref[s, low : low + 2 * W], g_ref[s, HEAD + low : HEAD + low + 2 * W]]
        built = dot(pick, jnp.concatenate(rows, axis=0)).astype(BF16)
        for c in range(3):
            xb[c, t + 2] = built[c * 64 : (c + 1) * 64]
    add_taps((pre, None), [x for x in TAPS if x[1] == 0], lambda b, c: xb.at[c], k1)


def early_kernel(g_ref, h_ref, k1, pre_ref, xb, pre, edge_ref):
    picks = [window_pick(b) for b in range(3)]
    for b in range(3):
        edge_ref[b] = picks[b][64:, 96:]
    own = jnp.concatenate([picks[1][:, :96], picks[2][:, :96]], axis=0)
    for i in range(6):
        xb[i, 0:2] = jnp.zeros((2, 64, C), BF16)
    for t in range(T):
        built = dot(own, jnp.concatenate(frame_rows(g_ref, h_ref, t), axis=0)).astype(BF16)
        for i in range(6):
            xb[i, t + 2] = built[i * 64 : (i + 1) * 64]
    taps = [x for x in TAPS if x[1] != 0]
    add_taps((pre, pre_ref), taps, lambda b, c: xb.at[b * 3 + c - 3], k1)


SPILL = 16


def clip_pick(b, c, rows, width, first):
    m, n = iota((rows, 64), 0), iota((rows, 64), 1)
    h, v = div(m, width), first + mod(m, width)
    k, col = div(n, W), column(mod(n, W))
    hit = (h == k + b) & (v == col + c) & (v < W + 2)
    if b != 1:
        hit = hit & jnp.logical_not((lax.axis_index("ha") == HA - 1) & (k == (3 if b == 0 else 2)))
    if c != 1:
        hit = hit & jnp.logical_not((lax.axis_index("wa") == WA - 1) & (col == (15 if c == 0 else 14)))
    return onehot(hit)


def middle_kernel(
    g_ref, h_ref, w_ref, k1, kdt, pre_ref, gp, act, cu, pre, act32, fix
):
    ta, last_h, last_w = lax.axis_index("ta"), lax.axis_index("ha") == HA - 1, lax.axis_index("wa") == WA - 1
    cot = 2 * F * W

    edges = w_ref[...].reshape(T * 16, C)
    m, n = iota((64, T * 16), 0), iota((64, T * 16), 1)
    t, k, e = div(m, 8), mod(div(m, 2), 4), mod(m, 2)
    total = None
    for i, (a, b, c) in enumerate(TAPS):
        if c == 0:
            continue
        hit = (n == (t - 2 + a) * 16 + (k + b) * 2 + e + (c - 2)) & (e + c >= 2)
        if b != 1:
            hit = hit & jnp.logical_not(last_h & (k == (3 if b == 0 else 2)))
        if c == 2:
            hit = hit & jnp.logical_not(last_w & (e == 0))
        y = dot(dot(onehot(hit), edges).astype(BF16), k1[i * C : (i + 1) * C])
        total = y if total is None else total + y
    fix[...] = total

    m, n = iota((144, 48), 0), iota((144, 48), 1)
    (b, c), place = third(div(m, 16)), mod(m, 16)
    kk, mm = div(place, 8), mod(place, 8)
    r, q = kk + jnp.where(b < 2, 1, 0), mm + jnp.where(c < 2, 1, 0)
    source = jnp.where(q == 8, 44 + r, r * 8 + q)
    out_h = last_h & (b == 0) & (kk == 1)
    out_w = last_w & (c == 0) & (mm == 7)
    pick = onehot((n == source) & jnp.logical_not(out_h | out_w))
    for i in range(9):
        cu[i, TA] = jnp.zeros((16, C), BF16)
    for j in range(TA):
        rows = jnp.concatenate(
            [g_ref[j, cot : cot + 16], h_ref[j, cot : cot + 16], w_ref[2 * j]], axis=0
        )
        built = dot(pick, rows).astype(BF16)
        for i in range(9):
            cu[i, j] = built[i * 16 : (i + 1) * 16]

    last = iota((8, C), 0) == 7
    for te in range(2):
        for ke in range(2):
            for ce in range(2):
                total = None
                for i, (a, b, c) in enumerate(TAPS):
                    if (a == 1, b == 1, c == 1) != (te == 1, ke == 1, ce == 1):
                        continue
                    ja = 1 if a < 2 else 0
                    y = dot(cu[b * 3 + c, ja : ja + 4].reshape(64, C), kdt[i * C : (i + 1) * C])
                    total = y if total is None else total + y
                for j in range(4):
                    for kk in range(2):
                        t, k = 2 * j + te, 2 * kk + ke
                        spot = t * 64 + k * W + ce * 8
                        late = (t * 4 + k) * 2 + ce
                        x = pre_ref[spot : spot + 8] + jnp.where(last, fix[late : late + 1], 0.0)
                        s = 1.0 / (1.0 + jnp.exp(-x))
                        at = (j * 2 + kk) * 8
                        g = total[at : at + 8]
                        act32[te * 4 + ke * 2 + ce, at : at + 8] = x * s
                        pre[spot : spot + 8] = g * s * (1.0 + x * (1.0 - s))
    gp[0:2] = jnp.zeros((2, 64, C), BF16)
    gp[2 : T + 2] = pre[...].astype(BF16).reshape(T, 64, C)
    gp[T + 2 : T + 4] = jnp.zeros((2, 64, C), BF16)
    act[...] = act32[...].astype(BF16)


def main_kernel(
    w_ref, xa_ref, xb_ref, edge_ref, gp, act, cu, mine_ref, other_ref, xc, tt
):
    ta, core = lax.axis_index("ta"), lax.rem(lax.axis_index("ha"), 2)

    share = onehot(iota((SHARE, C), 1) == iota((SHARE, C), 0) + ta * SHARE)
    turned = dot_t(share, gp[...].reshape((T + 4) * 64, C))
    left = jnp.concatenate(
        [turned[:, (2 - a) * 64 : (2 - a + T + 2) * 64] for a in range(3)], axis=0
    ).astype(BF16)
    late = edge_ref[...].reshape(6 * 64, 16)
    windows = [xa_ref.at[i] if i < 3 else xb_ref.at[i - 3] for i in range(9)]
    for i in range(6):
        xc[i, 0:2] = jnp.zeros((2, 64, C), BF16)
    for t in range(T):
        built = dot(late, w_ref[t]).astype(BF16)
        for i in range(6):
            base = windows[i // 2 * 3 + i % 2 + 1]
            xc[i, t + 2] = base[t + 2] + built[i * 64 : (i + 1) * 64]
    upper, lower = {}, {}
    for bc in range(9):
        x = windows[bc] if bc % 3 == 0 else xc.at[bc // 3 * 2 + bc % 3 - 1]
        y = dot(left, x[...].reshape((T + 2) * 64, C))
        for a in range(3):
            upper[a * 9 + bc] = y[a * SHARE : (a + 1) * SHARE]
    cots = {}
    for bc in range(9):
        for ja in range(2):
            cots[bc, ja] = dot_t(share, cu[bc, ja : ja + 4].reshape(64, C)).astype(BF16)
    for kind in range(8):
        taps = [
            (i, cots[b * 3 + c, 1 if a < 2 else 0])
            for i, (a, b, c) in enumerate(TAPS)
            if (a == 1) * 4 + (b == 1) * 2 + (c == 1) == kind
        ]
        y = dot(jnp.concatenate([x for _, x in taps], axis=0), act[kind])
        for place, (i, _) in enumerate(taps):
            lower[i] = y[place * SHARE : (place + 1) * SHARE]
    for i in range(27):
        both = jnp.concatenate([upper[i], lower[i]], axis=0).astype(BF16)
        tt[i * C : (i + 1) * C] = both.T.astype(F32)
    tt[27 * C :] = jnp.zeros((8, 2 * SHARE), F32)

    def cut(out_ref, parity):
        for x in range(HA // 2):
            for w in range(WA):
                first = ((x * 2 + parity) * WA + w) * PART
                spot = (x * WA + w) * SLOT
                out_ref[spot : spot + SLOT] = tt[first : first + SLOT].astype(BF16)

    for parity in range(2):

        @pl.when(core == parity)
        def _(parity=parity):
            cut(mine_ref, parity)
            cut(other_ref, 1 - parity)


MAIN = (R + 2) * W
WIDE = MAIN + SPILL


def clip_kernel(gp, k1t, own_ref, past_ref, spill_ref, yb, acc):
    later = gp[pl.ds(2 + F * lax.axis_index("ta"), F + 2)]
    for i in range(9):
        b, c = i // 3, i % 3
        pick = jnp.concatenate([clip_pick(b, c, MAIN, W, 0), clip_pick(b, c, SPILL, 2, W)], axis=0)
        for t in range(F + 2):
            yb[i, t] = dot(pick, later[t]).astype(BF16)
    for i, (a, b, c) in enumerate(TAPS):
        x = yb[b * 3 + c, 2 - a : 2 - a + F].reshape(F * WIDE, C)
        y = dot(x, k1t[i * C : (i + 1) * C])
        if i == 0:
            acc[...] = y
        else:
            acc[...] += y
    for f in range(F):
        own_ref[f] = acc[f * WIDE : f * WIDE + R * W]
        past_ref[f] = acc[f * WIDE + R * W : f * WIDE + MAIN].astype(BF16)
        spill_ref[f] = acc[f * WIDE + MAIN : (f + 1) * WIDE].astype(BF16)


def spilled(spill, h):
    place = iota((8, C), 0)
    first, second = spill[2 * h : 2 * h + 1], spill[2 * h + 1 : 2 * h + 2]
    return jnp.where(place == 0, first, jnp.where(place == 1, second, 0.0))


STAGES = 4


def join_kernel(mine_ref, other_ref, after_ref, out_ref, joined, sems):
    rows = PEERS * SLOT // STAGES
    copies = []
    for i in range(STAGES):
        part = pl.ds(i * rows, rows)
        joined[part] = mine_ref[part] + other_ref[part]
        copies.append(pltpu.make_async_copy(joined.at[part], out_ref.at[part], sems.at[i]))
        copies[-1].start()
    for copy in copies:
        copy.wait()


def finish_kernel(
    parts_ref, own_ref, spill_ref, past_ref, corner_ref, clip_ref, conv_ref, down_ref
):
    for f in range(F):
        spill, corner = spill_ref[f].astype(F32), corner_ref[f].astype(F32)
        past = past_ref[f].astype(F32)
        for h in range(R):
            at = h * W
            low = own_ref[f, at : at + 8] + spilled(spill, h)
            high = own_ref[f, at + 8 : at + W]
            if h < 2:
                low += past[at : at + 8] + spilled(corner, R + h)
                high += past[at + 8 : at + W]
            clip_ref[f, at : at + W] = jnp.concatenate([low, high], axis=0).astype(BF16)
    total = parts_ref[0].astype(F32)
    for i in range(1, PEERS):
        total += parts_ref[i].astype(F32)
    total = jnp.concatenate([total, jnp.zeros((128 - SLOT, 2 * SHARE), F32)], axis=0).T
    conv_ref[...] = total[:SHARE, :PART]
    down_ref[...] = total[SHARE:, :PART]


def whole():
    return pl.BlockSpec(memory_space=pltpu.VMEM)


def call(kernel, outs, specs, scratch, flops, name, out=None):
    return pl.pallas_call(
        kernel,
        out_shape=outs,
        in_specs=specs,
        out_specs=jax.tree.map(lambda _: out or whole(), outs),
        scratch_shapes=scratch,
        compiler_params=pltpu.CompilerParams(vmem_limit_bytes=VMEM_BYTES),
        cost_estimate=pl.CostEstimate(flops=flops, bytes_accessed=10_000, transcendentals=0),
        name=name,
    )


def shape(dims, dtype=BF16):
    return jax.ShapeDtypeStruct(dims, dtype)


def on_chip(dims, dtype=BF16):
    return pltpu.VMEM(dims, dtype)


def in_hbm(x):
    return pltpu.with_memory_space_constraint(x, pltpu.HBM)


def in_vmem(x):
    return pltpu.with_memory_space_constraint(x, pltpu.VMEM)


def shift(x, axis, by):
    count = lax.axis_size(axis)
    return lax.ppermute(x, axis, [(i, (i + by) % count) for i in range(count)])


def local(clip, conv_weight, down_weight, out_cotangent):
    anywhere = pl.BlockSpec(memory_space=pl.ANY)
    dma = pltpu.SemaphoreType.DMA
    packed = call(
        pack_kernel, shape((BLOCK, C)), [anywhere] * 2, [dma((5,))], 10**5, "pack"
    )(in_hbm(clip.reshape(2 * F, 2 * W, C)), in_hbm(out_cotangent.reshape(-1, C)))
    around = [shift(packed, "ta", by) for by in (1, 2, 3)]
    weight = on_chip((27 * C, C))
    k1, k1t, kdt = call(
        load_kernel,
        [weight] * 3,
        [anywhere] * 3,
        [pltpu.VMEM((27 * C, C), BF16), dma((9,)), dma((9,))],
        4 * 10**9,
        "load",
    )(packed, in_hbm(conv_weight), in_hbm(down_weight))
    k1, k1t, kdt = in_vmem(k1), in_vmem(k1t), in_vmem(kdt)
    head = call(
        head_kernel,
        shape((TA, HEAD, C)),
        [whole()] * 4 + [anywhere],
        [],
        10**5,
        "head",
    )(packed, *around, k1t)
    h = shift(head, "ha", -1)
    g, xa, pre = call(
        own_kernel,
        [shape((TA, BLOCK, C)), on_chip((3, T + 2, 64, C)), on_chip((T * 64, C), F32)],
        [whole()] * 4 + [anywhere, whole()],
        [],
        3 * 10**9,
        "own",
    )(packed, *around, head, k1)
    xa, pre = in_vmem(xa), in_vmem(pre)
    w = call(edge_kernel, shape((T, 16, C)), [whole()] * 2, [], 10**7, "edge")(g, h)
    w = shift(w, "wa", -1)
    xb, pre, edge = call(
        early_kernel,
        [on_chip((6, T + 2, 64, C)), on_chip((T * 64, C), F32), on_chip((3, 128, 16))],
        [whole()] * 4,
        [],
        3 * 10**9,
        "early",
    )(g, h, k1, pre)
    xb, pre, edge = in_vmem(xb), in_vmem(pre), in_vmem(edge)
    gp, act, cu = call(
        middle_kernel,
        [
            on_chip((T + 4, 64, C)),
            on_chip((8, 64, C)),
            on_chip((9, TA + 1, 16, C)),
        ],
        [whole()] * 6,
        [
            pltpu.VMEM((T * 64, C), F32),
            pltpu.VMEM((8, 64, C), F32),
            pltpu.VMEM((64, C), F32),
        ],
        3 * 10**9,
        "middle",
    )(g, h, w, k1, kdt, pre)
    gp, act, cu = in_vmem(gp), in_vmem(act), in_vmem(cu)
    mine, other = call(
        main_kernel,
        [shape((PEERS * SLOT, 2 * SHARE)), shape((PEERS * SLOT, 2 * SHARE))],
        [whole()] * 7,
        [pltpu.VMEM((6, T + 2, 64, C), BF16), pltpu.VMEM((27 * C + 8, 2 * SHARE), F32)],
        5 * 10**9,
        "main",
    )(w, xa, xb, edge, gp, act, cu)
    other = lax.ppermute(other, "ha", [(i, i ^ 1) for i in range(HA)])
    own, past, spill = call(
        clip_kernel,
        [shape((F, R * W, C), F32), shape((F, 2 * W, C)), shape((F, SPILL, C))],
        [whole()] * 2,
        [pltpu.VMEM((9, F + 2, WIDE, C), BF16), pltpu.VMEM((F * WIDE, C), F32)],
        10**9,
        "clip",
    )(gp, k1t)
    pair = call(
        join_kernel,
        shape((PEERS * SLOT, 2 * SHARE)),
        [whole(), whole(), anywhere],
        [pltpu.VMEM((PEERS * SLOT, 2 * SHARE), BF16), dma((STAGES,))],
        10**6,
        "join",
        anywhere,
    )(mine, other, own)
    pairs = [(i * WA + j, (i + 1) % HA * WA + (j + 1) % WA) for i in range(HA) for j in range(WA)]
    corner = lax.ppermute(spill, ("ha", "wa"), pairs)
    spill = shift(spill, "wa", 1)
    past = shift(past, "ha", 1)
    groups = [[i * WA + w for i in range(c, HA, 2) for w in range(WA)] for c in range(2)]
    parts = lax.all_to_all(pair, ("ha", "wa"), 0, 0, axis_index_groups=groups, tiled=True)
    grad_clip, grad_conv, grad_down = call(
        finish_kernel,
        [shape((F, R * W, C)), shape((SHARE, PART), F32), shape((SHARE, PART), F32)],
        [whole()] * 5,
        [],
        10**6,
        "finish",
    )(parts.reshape(PEERS, SLOT, 2 * SHARE), own, spill, past, corner)
    grad_clip = grad_clip.reshape(F, R, W, C)
    return (grad_clip, grad_conv.T, grad_down.T)


def solution(mesh):
    return jax.shard_map(
        local,
        mesh=mesh,
        in_specs=(P("ta", "ha", "wa", None), P(), P(), P("ta", "ha", "wa", None)),
        out_specs=(P("ta", "ha", "wa", None), P(("ha", "wa"), "ta"), P(("ha", "wa"), "ta")),
        check_vma=False,
    )
```

```python
import functools

import jax
import jax.numpy as jnp
from jax import lax
from jax.experimental import pallas as pl
from jax.experimental.pallas import tpu as pltpu
from jax.sharding import PartitionSpec as P

F, R, W, C = 2, 4, 16, 256
TA, HA, WA = 4, 8, 8
T = TA * F
HEAD = 2 * F * W + (R // 2) * (W // 2)
BLOCK = F * R * W + (R // 2) * (W // 2)
SHARE = C // TA
PART = 27 * C // (HA * WA)
SLOT = 112
PEERS = HA * WA // 2
HALF = PEERS * SLOT // 2
TAPS = [(a, b, c) for a in range(3) for b in range(3) for c in range(3)]
BF16, F32 = jnp.bfloat16, jnp.float32
VMEM_BYTES = 28 * 1024 * 1024


def iota(shape, dim):
    return lax.broadcasted_iota(jnp.int32, shape, dim)


def onehot(hit):
    return jnp.where(hit, 1.0, 0.0).astype(F32).astype(BF16)


def div(x, n):
    return lax.shift_right_logical(x, n.bit_length() - 1)


def mod(x, n):
    return lax.bitwise_and(x, n - 1)


def third(x):
    high = jnp.where(x >= 3, 1, 0) + jnp.where(x >= 6, 1, 0)
    return high, x - 3 * high


def dot(x, y):
    return jnp.dot(x, y, preferred_element_type=F32)


def dot_t(x, y):
    return lax.dot_general(x, y, (((1,), (1,)), ((), ())), preferred_element_type=F32)


def column(order):
    return jnp.where(order < W // 2, 2 * order, 2 * (order - W // 2) + 1)


def frame_rows(g_ref, h_ref, t):
    s, f = t // F, t % F
    low = 2 * W * f
    return [
        g_ref[s, low : low + 2 * W],
        g_ref[s, HEAD + low : HEAD + low + 2 * W],
        h_ref[s, low : low + 2 * W],
    ]


def edge_kernel(g_ref, h_ref, out_ref):
    cot = 2 * F * W
    m, n = iota((16, 128), 0), iota((16, 128), 1)
    source = jnp.where(m < 12, div(m, 2) * W + mod(m, 2), jnp.where(m < 14, 96 + (m - 12) * 8, 112))
    pick = onehot((n == source) & (m < 15))
    for t in range(T):
        s = t // F
        rows = frame_rows(g_ref, h_ref, t) + [g_ref[s, cot : cot + 16], h_ref[s, cot : cot + 16]]
        out_ref[t] = dot(pick, jnp.concatenate(rows, axis=0)).astype(BF16)


def pack_kernel(clip_ref, cot_ref, out_ref, sems):
    half = 2 * W
    copies = []
    for f in range(F):
        for part in range(2):
            spot = part * HEAD + f * half
            copies.append((clip_ref.at[2 * f + part], out_ref.at[pl.ds(spot, half)]))
    copies.append((cot_ref, out_ref.at[pl.ds(2 * F * W, 16)]))
    copies = [pltpu.make_async_copy(x, y, sems.at[i]) for i, (x, y) in enumerate(copies)]
    for copy in copies:
        copy.start()
    for copy in copies:
        copy.wait()


def head_kernel(own_ref, one_ref, two_ref, three_ref, after_ref, head_ref):
    for back, ref in enumerate((own_ref, one_ref, two_ref, three_ref)):
        head_ref[lax.rem(lax.axis_index("ta") + TA - back, TA)] = ref[:HEAD]


def fetch(source, target, sems):
    step = 3 * C
    parts = [pl.ds(i * step, step) for i in range(9)]
    copies = [
        pltpu.make_async_copy(source.at[part], target.at[part], sems.at[i])
        for i, part in enumerate(parts)
    ]
    for copy in copies:
        copy.start()
    return copies


def turn(copies, plain, turned):
    for i in range(27):
        if i % 3 == 0:
            copies[i // 3].wait()
        turned[i * C : (i + 1) * C] = plain[i * C : (i + 1) * C].T


def load_kernel(after_ref, k1_ref, kd_ref, k1, k1t, kdt, kd, sems1, semsd):
    first, second = fetch(k1_ref, k1, sems1), fetch(kd_ref, kd, semsd)
    turn(first, k1, k1t)
    turn(second, kd, kdt)


def window_pick(b):
    last_h, last_w = lax.axis_index("ha") == HA - 1, lax.axis_index("wa") == WA - 1
    m, n = iota((192, 112), 0), iota((192, 112), 1)
    c, place = div(m, 64), mod(m, 64)
    k, col = div(place, W), column(mod(place, W))
    row, v = k + b, col + c
    source = jnp.where(v < W, row * W + v, 96 + row * 2 + v - W)
    out = last_w & (((c == 0) & (col == 15)) | ((c == 2) & (col == 14)))
    if b != 1:
        out = out | (last_h & (k == (3 if b == 0 else 2)))
    return onehot((n == source) & jnp.logical_not(out))


def add_taps(total, taps, x, k1):
    for first, (a, b, c) in enumerate(taps):
        i = (a * 3 + b) * 3 + c
        y = dot(x(b, c)[a : a + T].reshape(T * 64, C), k1[i * C : (i + 1) * C])
        if first == 0 and total[1] is None:
            total[0][...] = y
        elif first == 0:
            total[0][...] = total[1][...] + y
        else:
            total[0][...] += y


def own_kernel(
    own_ref, one_ref, two_ref, three_ref, after_ref, k1, g_ref, xb, pre
):
    for back, ref in enumerate((own_ref, one_ref, two_ref, three_ref)):
        g_ref[lax.rem(lax.axis_index("ta") + TA - back, TA)] = ref[...]
    pick = window_pick(0)[:, :64]
    for c in range(3):
        xb[c, 0:2] = jnp.zeros((2, 64, C), BF16)
    for t in range(T):
        s, low = t // F, 2 * W * (t % F)
        rows = [g_ref[s, low : low + 2 * W], g_ref[s, HEAD + low : HEAD + low + 2 * W]]
        built = dot(pick, jnp.concatenate(rows, axis=0)).astype(BF16)
        for c in range(3):
            xb[c, t + 2] = built[c * 64 : (c + 1) * 64]
    add_taps((pre, None), [x for x in TAPS if x[1] == 0], lambda b, c: xb.at[c], k1)


def early_kernel(g_ref, h_ref, k1, pre_ref, xb, pre, edge_ref):
    picks = [window_pick(b) for b in range(3)]
    for b in range(3):
        edge_ref[b] = picks[b][64:, 96:]
    own = jnp.concatenate([picks[1][:, :96], picks[2][:, :96]], axis=0)
    for i in range(6):
        xb[i, 0:2] = jnp.zeros((2, 64, C), BF16)
    for t in range(T):
        built = dot(own, jnp.concatenate(frame_rows(g_ref, h_ref, t), axis=0)).astype(BF16)
        for i in range(6):
            xb[i, t + 2] = built[i * 64 : (i + 1) * 64]
    taps = [x for x in TAPS if x[1] != 0]
    add_taps((pre, pre_ref), taps, lambda b, c: xb.at[b * 3 + c - 3], k1)


SPILL = 16


def clip_pick(b, c, rows, width, first):
    m, n = iota((rows, 64), 0), iota((rows, 64), 1)
    h, v = div(m, width), first + mod(m, width)
    k, col = div(n, W), column(mod(n, W))
    hit = (h == k + b) & (v == col + c) & (v < W + 2)
    if b != 1:
        hit = hit & jnp.logical_not((lax.axis_index("ha") == HA - 1) & (k == (3 if b == 0 else 2)))
    if c != 1:
        hit = hit & jnp.logical_not((lax.axis_index("wa") == WA - 1) & (col == (15 if c == 0 else 14)))
    return onehot(hit)


def middle_kernel(
    g_ref, h_ref, w_ref, k1, kdt, pre_ref, gp, act, cu, pre, act32, fix
):
    ta, last_h, last_w = lax.axis_index("ta"), lax.axis_index("ha") == HA - 1, lax.axis_index("wa") == WA - 1
    cot = 2 * F * W

    edges = w_ref[...].reshape(T * 16, C)
    m, n = iota((64, T * 16), 0), iota((64, T * 16), 1)
    t, k, e = div(m, 8), mod(div(m, 2), 4), mod(m, 2)
    total = None
    for i, (a, b, c) in enumerate(TAPS):
        if c == 0:
            continue
        hit = (n == (t - 2 + a) * 16 + (k + b) * 2 + e + (c - 2)) & (e + c >= 2)
        if b != 1:
            hit = hit & jnp.logical_not(last_h & (k == (3 if b == 0 else 2)))
        if c == 2:
            hit = hit & jnp.logical_not(last_w & (e == 0))
        y = dot(dot(onehot(hit), edges).astype(BF16), k1[i * C : (i + 1) * C])
        total = y if total is None else total + y
    fix[...] = total

    m, n = iota((144, 48), 0), iota((144, 48), 1)
    (b, c), place = third(div(m, 16)), mod(m, 16)
    kk, mm = div(place, 8), mod(place, 8)
    r, q = kk + jnp.where(b < 2, 1, 0), mm + jnp.where(c < 2, 1, 0)
    source = jnp.where(q == 8, 44 + r, r * 8 + q)
    out_h = last_h & (b == 0) & (kk == 1)
    out_w = last_w & (c == 0) & (mm == 7)
    pick = onehot((n == source) & jnp.logical_not(out_h | out_w))
    for i in range(9):
        cu[i, TA] = jnp.zeros((16, C), BF16)
    for j in range(TA):
        rows = jnp.concatenate(
            [g_ref[j, cot : cot + 16], h_ref[j, cot : cot + 16], w_ref[2 * j]], axis=0
        )
        built = dot(pick, rows).astype(BF16)
        for i in range(9):
            cu[i, j] = built[i * 16 : (i + 1) * 16]

    last = iota((8, C), 0) == 7
    for te in range(2):
        for ke in range(2):
            for ce in range(2):
                total = None
                for i, (a, b, c) in enumerate(TAPS):
                    if (a == 1, b == 1, c == 1) != (te == 1, ke == 1, ce == 1):
                        continue
                    ja = 1 if a < 2 else 0
                    y = dot(cu[b * 3 + c, ja : ja + 4].reshape(64, C), kdt[i * C : (i + 1) * C])
                    total = y if total is None else total + y
                for j in range(4):
                    for kk in range(2):
                        t, k = 2 * j + te, 2 * kk + ke
                        spot = t * 64 + k * W + ce * 8
                        late = (t * 4 + k) * 2 + ce
                        x = pre_ref[spot : spot + 8] + jnp.where(last, fix[late : late + 1], 0.0)
                        s = 1.0 / (1.0 + jnp.exp(-x))
                        at = (j * 2 + kk) * 8
                        g = total[at : at + 8]
                        act32[te * 4 + ke * 2 + ce, at : at + 8] = x * s
                        pre[spot : spot + 8] = g * s * (1.0 + x * (1.0 - s))
    gp[0:2] = jnp.zeros((2, 64, C), BF16)
    gp[2 : T + 2] = pre[...].astype(BF16).reshape(T, 64, C)
    gp[T + 2 : T + 4] = jnp.zeros((2, 64, C), BF16)
    act[...] = act32[...].astype(BF16)


def main_kernel(
    w_ref, xa_ref, xb_ref, edge_ref, gp, act, cu, mine_ref, mine2_ref, other_ref, other2_ref, xc, tt
):
    ta, core = lax.axis_index("ta"), lax.rem(lax.axis_index("ha"), 2)

    share = onehot(iota((SHARE, C), 1) == iota((SHARE, C), 0) + ta * SHARE)
    turned = dot_t(share, gp[...].reshape((T + 4) * 64, C))
    left = jnp.concatenate(
        [turned[:, (2 - a) * 64 : (2 - a + T + 2) * 64] for a in range(3)], axis=0
    ).astype(BF16)
    late = edge_ref[...].reshape(6 * 64, 16)
    windows = [xa_ref.at[i] if i < 3 else xb_ref.at[i - 3] for i in range(9)]
    for i in range(6):
        xc[i, 0:2] = jnp.zeros((2, 64, C), BF16)
    for t in range(T):
        built = dot(late, w_ref[t]).astype(BF16)
        for i in range(6):
            base = windows[i // 2 * 3 + i % 2 + 1]
            xc[i, t + 2] = base[t + 2] + built[i * 64 : (i + 1) * 64]
    upper, lower = {}, {}
    for bc in range(9):
        x = windows[bc] if bc % 3 == 0 else xc.at[bc // 3 * 2 + bc % 3 - 1]
        y = dot(left, x[...].reshape((T + 2) * 64, C))
        for a in range(3):
            upper[a * 9 + bc] = y[a * SHARE : (a + 1) * SHARE]
    cots = {}
    for bc in range(9):
        for ja in range(2):
            cots[bc, ja] = dot_t(share, cu[bc, ja : ja + 4].reshape(64, C)).astype(BF16)
    for kind in range(8):
        taps = [
            (i, cots[b * 3 + c, 1 if a < 2 else 0])
            for i, (a, b, c) in enumerate(TAPS)
            if (a == 1) * 4 + (b == 1) * 2 + (c == 1) == kind
        ]
        y = dot(jnp.concatenate([x for _, x in taps], axis=0), act[kind])
        for place, (i, _) in enumerate(taps):
            lower[i] = y[place * SHARE : (place + 1) * SHARE]
    for i in range(27):
        both = jnp.concatenate([upper[i], lower[i]], axis=0).astype(BF16)
        tt[i * C : (i + 1) * C] = both.T.astype(F32)
    tt[27 * C :] = jnp.zeros((8, 2 * SHARE), F32)

    def cut(out_refs, parity):
        for x in range(HA // 2):
            for w in range(WA):
                first = ((x * 2 + parity) * WA + w) * PART
                spot = (x * WA + w) * SLOT
                ref = out_refs[spot // HALF]
                spot %= HALF
                ref[spot : spot + SLOT] = tt[first : first + SLOT].astype(BF16)

    for parity in range(2):

        @pl.when(core == parity)
        def _(parity=parity):
            cut((mine_ref, mine2_ref), parity)
            cut((other_ref, other2_ref), 1 - parity)


MAIN = (R + 2) * W
WIDE = MAIN + SPILL


def clip_kernel(gp, k1t, own_ref, past_ref, spill_ref, yb, acc):
    later = gp[pl.ds(2 + F * lax.axis_index("ta"), F + 2)]
    for i in range(9):
        b, c = i // 3, i % 3
        pick = jnp.concatenate([clip_pick(b, c, MAIN, W, 0), clip_pick(b, c, SPILL, 2, W)], axis=0)
        for t in range(F + 2):
            yb[i, t] = dot(pick, later[t]).astype(BF16)
    for i, (a, b, c) in enumerate(TAPS):
        x = yb[b * 3 + c, 2 - a : 2 - a + F].reshape(F * WIDE, C)
        y = dot(x, k1t[i * C : (i + 1) * C])
        if i == 0:
            acc[...] = y
        else:
            acc[...] += y
    for f in range(F):
        own_ref[f] = acc[f * WIDE : f * WIDE + R * W]
        past_ref[f] = acc[f * WIDE + R * W : f * WIDE + MAIN].astype(BF16)
        spill_ref[f] = acc[f * WIDE + MAIN : (f + 1) * WIDE].astype(BF16)


def spilled(spill, h):
    place = iota((8, C), 0)
    first, second = spill[2 * h : 2 * h + 1], spill[2 * h + 1 : 2 * h + 2]
    return jnp.where(place == 0, first, jnp.where(place == 1, second, 0.0))


STAGES = 2


def join_kernel(part, mine_ref, other_ref, after_ref, out_ref, joined, sems):
    rows = HALF // STAGES
    copies = []
    for i in range(STAGES):
        spot = pl.ds(i * rows, rows)
        joined[spot] = mine_ref[spot] + other_ref[spot]
        there = pl.ds(part * HALF + i * rows, rows)
        copies.append(pltpu.make_async_copy(joined.at[spot], out_ref.at[there], sems.at[i]))
        copies[-1].start()
    for copy in copies:
        copy.wait()


def finish_kernel(
    parts_ref, own_ref, spill_ref, past_ref, corner_ref, clip_ref, conv_ref, down_ref
):
    for f in range(F):
        spill, corner = spill_ref[f].astype(F32), corner_ref[f].astype(F32)
        past = past_ref[f].astype(F32)
        for h in range(R):
            at = h * W
            low = own_ref[f, at : at + 8] + spilled(spill, h)
            high = own_ref[f, at + 8 : at + W]
            if h < 2:
                low += past[at : at + 8] + spilled(corner, R + h)
                high += past[at + 8 : at + W]
            clip_ref[f, at : at + W] = jnp.concatenate([low, high], axis=0).astype(BF16)
    total = parts_ref[0].astype(F32)
    for i in range(1, PEERS):
        total += parts_ref[i].astype(F32)
    total = jnp.concatenate([total, jnp.zeros((128 - SLOT, 2 * SHARE), F32)], axis=0).T
    conv_ref[...] = total[:SHARE, :PART]
    down_ref[...] = total[SHARE:, :PART]


def whole():
    return pl.BlockSpec(memory_space=pltpu.VMEM)


def call(kernel, outs, specs, scratch, flops, name, out=None, aliases={}):
    return pl.pallas_call(
        kernel,
        out_shape=outs,
        in_specs=specs,
        out_specs=jax.tree.map(lambda _: out or whole(), outs),
        scratch_shapes=scratch,
        input_output_aliases=aliases,
        compiler_params=pltpu.CompilerParams(vmem_limit_bytes=VMEM_BYTES),
        cost_estimate=pl.CostEstimate(flops=flops, bytes_accessed=10_000, transcendentals=0),
        name=name,
    )


def shape(dims, dtype=BF16):
    return jax.ShapeDtypeStruct(dims, dtype)


def on_chip(dims, dtype=BF16):
    return pltpu.VMEM(dims, dtype)


def in_hbm(x):
    return pltpu.with_memory_space_constraint(x, pltpu.HBM)


def in_vmem(x):
    return pltpu.with_memory_space_constraint(x, pltpu.VMEM)


def shift(x, axis, by):
    count = lax.axis_size(axis)
    return lax.ppermute(x, axis, [(i, (i + by) % count) for i in range(count)])


def local(clip, conv_weight, down_weight, out_cotangent):
    anywhere = pl.BlockSpec(memory_space=pl.ANY)
    dma = pltpu.SemaphoreType.DMA
    packed = call(
        pack_kernel, shape((BLOCK, C)), [anywhere] * 2, [dma((5,))], 10**5, "pack"
    )(in_hbm(clip.reshape(2 * F, 2 * W, C)), in_hbm(out_cotangent.reshape(-1, C)))
    around = [shift(packed, "ta", by) for by in (1, 2, 3)]
    weight = on_chip((27 * C, C))
    k1, k1t, kdt = call(
        load_kernel,
        [weight] * 3,
        [anywhere] * 3,
        [pltpu.VMEM((27 * C, C), BF16), dma((9,)), dma((9,))],
        4 * 10**9,
        "load",
    )(packed, in_hbm(conv_weight), in_hbm(down_weight))
    k1, k1t, kdt = in_vmem(k1), in_vmem(k1t), in_vmem(kdt)
    head = call(
        head_kernel,
        shape((TA, HEAD, C)),
        [whole()] * 4 + [anywhere],
        [],
        10**5,
        "head",
    )(packed, *around, k1t)
    h = shift(head, "ha", -1)
    g, xa, pre = call(
        own_kernel,
        [shape((TA, BLOCK, C)), on_chip((3, T + 2, 64, C)), on_chip((T * 64, C), F32)],
        [whole()] * 4 + [anywhere, whole()],
        [],
        3 * 10**9,
        "own",
    )(packed, *around, head, k1)
    xa, pre = in_vmem(xa), in_vmem(pre)
    w = call(edge_kernel, shape((T, 16, C)), [whole()] * 2, [], 10**7, "edge")(g, h)
    w = shift(w, "wa", -1)
    xb, pre, edge = call(
        early_kernel,
        [on_chip((6, T + 2, 64, C)), on_chip((T * 64, C), F32), on_chip((3, 128, 16))],
        [whole()] * 4,
        [],
        3 * 10**9,
        "early",
    )(g, h, k1, pre)
    xb, pre, edge = in_vmem(xb), in_vmem(pre), in_vmem(edge)
    gp, act, cu = call(
        middle_kernel,
        [
            on_chip((T + 4, 64, C)),
            on_chip((8, 64, C)),
            on_chip((9, TA + 1, 16, C)),
        ],
        [whole()] * 6,
        [
            pltpu.VMEM((T * 64, C), F32),
            pltpu.VMEM((8, 64, C), F32),
            pltpu.VMEM((64, C), F32),
        ],
        3 * 10**9,
        "middle",
    )(g, h, w, k1, kdt, pre)
    gp, act, cu = in_vmem(gp), in_vmem(act), in_vmem(cu)
    mine, mine2, other, other2 = call(
        main_kernel,
        [shape((HALF, 2 * SHARE))] * 4,
        [whole()] * 7,
        [pltpu.VMEM((6, T + 2, 64, C), BF16), pltpu.VMEM((27 * C + 8, 2 * SHARE), F32)],
        5 * 10**9,
        "main",
    )(w, xa, xb, edge, gp, act, cu)
    cores = [(i, i ^ 1) for i in range(HA)]
    other, other2 = lax.ppermute(other, "ha", cores), lax.ppermute(other2, "ha", cores)
    own, past, spill = call(
        clip_kernel,
        [shape((F, R * W, C), F32), shape((F, 2 * W, C)), shape((F, SPILL, C))],
        [whole()] * 2,
        [pltpu.VMEM((9, F + 2, WIDE, C), BF16), pltpu.VMEM((F * WIDE, C), F32)],
        10**9,
        "clip",
    )(gp, k1t)
    pair = own
    for part, (x, y) in enumerate(((mine, other), (mine2, other2))):
        pair = call(
            functools.partial(join_kernel, part),
            shape((PEERS * SLOT, 2 * SHARE)),
            [whole(), whole(), anywhere],
            [pltpu.VMEM((HALF, 2 * SHARE), BF16), dma((STAGES,))],
            10**6,
            "join" + str(part),
            anywhere,
            aliases={2: 0} if part else {},
        )(x, y, pair)
    pairs = [(i * WA + j, (i + 1) % HA * WA + (j + 1) % WA) for i in range(HA) for j in range(WA)]
    corner = lax.ppermute(spill, ("ha", "wa"), pairs)
    spill = shift(spill, "wa", 1)
    past = shift(past, "ha", 1)
    groups = [[i * WA + w for i in range(c, HA, 2) for w in range(WA)] for c in range(2)]
    parts = lax.all_to_all(pair, ("ha", "wa"), 0, 0, axis_index_groups=groups, tiled=True)
    grad_clip, grad_conv, grad_down = call(
        finish_kernel,
        [shape((F, R * W, C)), shape((SHARE, PART), F32), shape((SHARE, PART), F32)],
        [whole()] * 5,
        [],
        10**6,
        "finish",
    )(parts.reshape(PEERS, SLOT, 2 * SHARE), own, spill, past, corner)
    grad_clip = grad_clip.reshape(F, R, W, C)
    return (grad_clip, grad_conv.T, grad_down.T)


def solution(mesh):
    return jax.shard_map(
        local,
        mesh=mesh,
        in_specs=(P("ta", "ha", "wa", None), P(), P(), P("ta", "ha", "wa", None)),
        out_specs=(P("ta", "ha", "wa", None), P(("ha", "wa"), "ta"), P(("ha", "wa"), "ta")),
        check_vma=False,
    )
```

```python
import jax
import jax.numpy as jnp
from jax import lax
from jax.experimental import pallas as pl
from jax.experimental.pallas import tpu as pltpu
from jax.sharding import PartitionSpec as P

F, R, W, C = 2, 4, 16, 256
TA, HA, WA = 4, 8, 8
T = TA * F
HEAD = 2 * F * W + (R // 2) * (W // 2)
BLOCK = F * R * W + (R // 2) * (W // 2)
SHARE = C // TA
PART = 27 * C // (HA * WA)
SLOT = 112
PEERS = HA * WA // 2
TAPS = [(a, b, c) for a in range(3) for b in range(3) for c in range(3)]
BF16, F32 = jnp.bfloat16, jnp.float32
VMEM_BYTES = 28 * 1024 * 1024


def iota(shape, dim):
    return lax.broadcasted_iota(jnp.int32, shape, dim)


def onehot(hit):
    return jnp.where(hit, 1.0, 0.0).astype(F32).astype(BF16)


def div(x, n):
    return lax.shift_right_logical(x, n.bit_length() - 1)


def mod(x, n):
    return lax.bitwise_and(x, n - 1)


def third(x):
    high = jnp.where(x >= 3, 1, 0) + jnp.where(x >= 6, 1, 0)
    return high, x - 3 * high


def dot(x, y):
    return jnp.dot(x, y, preferred_element_type=F32)


def dot_t(x, y):
    return lax.dot_general(x, y, (((1,), (1,)), ((), ())), preferred_element_type=F32)


def column(order):
    return jnp.where(order < W // 2, 2 * order, 2 * (order - W // 2) + 1)


def frame_rows(g_ref, h_ref, t):
    s, f = t // F, t % F
    low = 2 * W * f
    return [
        g_ref[s, low : low + 2 * W],
        g_ref[s, HEAD + low : HEAD + low + 2 * W],
        h_ref[s, low : low + 2 * W],
    ]


def edge_kernel(g_ref, h_ref, out_ref):
    cot = 2 * F * W
    m, n = iota((16, 128), 0), iota((16, 128), 1)
    source = jnp.where(m < 12, div(m, 2) * W + mod(m, 2), jnp.where(m < 14, 96 + (m - 12) * 8, 112))
    pick = onehot((n == source) & (m < 15))
    for t in range(T):
        s = t // F
        rows = frame_rows(g_ref, h_ref, t) + [g_ref[s, cot : cot + 16], h_ref[s, cot : cot + 16]]
        out_ref[t] = dot(pick, jnp.concatenate(rows, axis=0)).astype(BF16)


def pack_kernel(clip_ref, cot_ref, out_ref, sems):
    half = 2 * W
    copies = []
    for f in range(F):
        for part in range(2):
            spot = part * HEAD + f * half
            copies.append((clip_ref.at[2 * f + part], out_ref.at[pl.ds(spot, half)]))
    copies.append((cot_ref, out_ref.at[pl.ds(2 * F * W, 16)]))
    copies = [pltpu.make_async_copy(x, y, sems.at[i]) for i, (x, y) in enumerate(copies)]
    for copy in copies:
        copy.start()
    for copy in copies:
        copy.wait()


def head_kernel(own_ref, one_ref, two_ref, three_ref, after_ref, head_ref):
    for back, ref in enumerate((own_ref, one_ref, two_ref, three_ref)):
        head_ref[lax.bitwise_xor(lax.axis_index("ta"), back)] = ref[:HEAD]


def fetch(source, target, sems):
    step = 3 * C
    parts = [pl.ds(i * step, step) for i in range(9)]
    copies = [
        pltpu.make_async_copy(source.at[part], target.at[part], sems.at[i])
        for i, part in enumerate(parts)
    ]
    for copy in copies:
        copy.start()
    return copies


def turn(copies, plain, turned):
    for i in range(27):
        if i % 3 == 0:
            copies[i // 3].wait()
        turned[i * C : (i + 1) * C] = plain[i * C : (i + 1) * C].T


def load_kernel(after_ref, k1_ref, kd_ref, k1, k1t, kdt, kd, sems1, semsd):
    first, second = fetch(k1_ref, k1, sems1), fetch(kd_ref, kd, semsd)
    turn(first, k1, k1t)
    turn(second, kd, kdt)


def window_pick(b):
    last_h, last_w = lax.axis_index("ha") == HA - 1, lax.axis_index("wa") == WA - 1
    m, n = iota((192, 112), 0), iota((192, 112), 1)
    c, place = div(m, 64), mod(m, 64)
    k, col = div(place, W), column(mod(place, W))
    row, v = k + b, col + c
    source = jnp.where(v < W, row * W + v, 96 + row * 2 + v - W)
    out = last_w & (((c == 0) & (col == 15)) | ((c == 2) & (col == 14)))
    if b != 1:
        out = out | (last_h & (k == (3 if b == 0 else 2)))
    return onehot((n == source) & jnp.logical_not(out))


def add_taps(total, taps, x, k1):
    for first, (a, b, c) in enumerate(taps):
        i = (a * 3 + b) * 3 + c
        y = dot(x(b, c)[a : a + T].reshape(T * 64, C), k1[i * C : (i + 1) * C])
        if first == 0 and total[1] is None:
            total[0][...] = y
        elif first == 0:
            total[0][...] = total[1][...] + y
        else:
            total[0][...] += y


def own_kernel(
    own_ref, one_ref, two_ref, three_ref, after_ref, k1, g_ref, xb, pre
):
    for back, ref in enumerate((own_ref, one_ref, two_ref, three_ref)):
        g_ref[lax.bitwise_xor(lax.axis_index("ta"), back)] = ref[...]
    pick = window_pick(0)[:, :64]
    for c in range(3):
        xb[c, 0:2] = jnp.zeros((2, 64, C), BF16)
    for t in range(T):
        s, low = t // F, 2 * W * (t % F)
        rows = [g_ref[s, low : low + 2 * W], g_ref[s, HEAD + low : HEAD + low + 2 * W]]
        built = dot(pick, jnp.concatenate(rows, axis=0)).astype(BF16)
        for c in range(3):
            xb[c, t + 2] = built[c * 64 : (c + 1) * 64]
    add_taps((pre, None), [x for x in TAPS if x[1] == 0], lambda b, c: xb.at[c], k1)


def early_kernel(g_ref, h_ref, k1, kdt, pre_ref, xb, pre, edge_ref, part, cu):
    picks = [window_pick(b) for b in range(3)]
    for b in range(3):
        edge_ref[b] = picks[b][64:, 96:]
    own = jnp.concatenate([picks[1][:, :96], picks[2][:, :96]], axis=0)
    for i in range(6):
        xb[i, 0:2] = jnp.zeros((2, 64, C), BF16)
    for t in range(T):
        built = dot(own, jnp.concatenate(frame_rows(g_ref, h_ref, t), axis=0)).astype(BF16)
        for i in range(6):
            xb[i, t + 2] = built[i * 64 : (i + 1) * 64]
    taps = [x for x in TAPS if x[1] != 0]
    add_taps((pre, pre_ref), taps, lambda b, c: xb.at[b * 3 + c - 3], k1)

    cot = 2 * F * W
    m, n = iota((48, 32), 0), iota((48, 32), 1)
    b, place = div(m, 16), mod(m, 16)
    kk, mm = div(place, 8), mod(place, 8)
    r = kk + jnp.where(b < 2, 1, 0)
    out = (lax.axis_index("ha") == HA - 1) & (b == 0) & (kk == 1)
    pick = onehot((n == r * 8 + mm) & jnp.logical_not(out))
    for b in range(3):
        cu[b, TA] = jnp.zeros((16, C), BF16)
    for j in range(TA):
        rows = jnp.concatenate([g_ref[j, cot : cot + 16], h_ref[j, cot : cot + 16]], axis=0)
        built = dot(pick, rows).astype(BF16)
        for b in range(3):
            cu[b, j] = built[b * 16 : (b + 1) * 16]
    for te in range(2):
        for ke in range(2):
            total = None
            for i, (a, b, c) in enumerate(TAPS):
                if (a == 1, b == 1, c) != (te == 1, ke == 1, 2):
                    continue
                ja = 1 if a < 2 else 0
                y = dot(cu[b, ja : ja + 4].reshape(64, C), kdt[i * C : (i + 1) * C])
                total = y if total is None else total + y
            part[te * 2 + ke] = total


SPILL = 16


def clip_pick(b, c, rows, width, first):
    m, n = iota((rows, 64), 0), iota((rows, 64), 1)
    h, v = div(m, width), first + mod(m, width)
    k, col = div(n, W), column(mod(n, W))
    hit = (h == k + b) & (v == col + c) & (v < W + 2)
    if b != 1:
        hit = hit & jnp.logical_not((lax.axis_index("ha") == HA - 1) & (k == (3 if b == 0 else 2)))
    if c != 1:
        hit = hit & jnp.logical_not((lax.axis_index("wa") == WA - 1) & (col == (15 if c == 0 else 14)))
    return onehot(hit)


def middle_kernel(
    g_ref, h_ref, w_ref, k1, kdt, pre_ref, part_ref, gp, act, cu, pre, act32, fix
):
    ta, last_h, last_w = lax.axis_index("ta"), lax.axis_index("ha") == HA - 1, lax.axis_index("wa") == WA - 1
    cot = 2 * F * W

    edges = w_ref[...].reshape(T * 16, C)
    m, n = iota((64, T * 16), 0), iota((64, T * 16), 1)
    t, k, e = div(m, 8), mod(div(m, 2), 4), mod(m, 2)
    total = None
    for i, (a, b, c) in enumerate(TAPS):
        if c == 0:
            continue
        hit = (n == (t - 2 + a) * 16 + (k + b) * 2 + e + (c - 2)) & (e + c >= 2)
        if b != 1:
            hit = hit & jnp.logical_not(last_h & (k == (3 if b == 0 else 2)))
        if c == 2:
            hit = hit & jnp.logical_not(last_w & (e == 0))
        y = dot(dot(onehot(hit), edges).astype(BF16), k1[i * C : (i + 1) * C])
        total = y if total is None else total + y
    fix[...] = total

    m, n = iota((144, 48), 0), iota((144, 48), 1)
    (b, c), place = third(div(m, 16)), mod(m, 16)
    kk, mm = div(place, 8), mod(place, 8)
    r, q = kk + jnp.where(b < 2, 1, 0), mm + jnp.where(c < 2, 1, 0)
    source = jnp.where(q == 8, 44 + r, r * 8 + q)
    out_h = last_h & (b == 0) & (kk == 1)
    out_w = last_w & (c == 0) & (mm == 7)
    pick = onehot((n == source) & jnp.logical_not(out_h | out_w))
    for i in range(9):
        cu[i, TA] = jnp.zeros((16, C), BF16)
    for j in range(TA):
        rows = jnp.concatenate(
            [g_ref[j, cot : cot + 16], h_ref[j, cot : cot + 16], w_ref[2 * j]], axis=0
        )
        built = dot(pick, rows).astype(BF16)
        for i in range(9):
            cu[i, j] = built[i * 16 : (i + 1) * 16]

    last = iota((8, C), 0) == 7
    for te in range(2):
        for ke in range(2):
            for ce in range(2):
                total = part_ref[te * 2 + ke] if ce == 0 else None
                for i, (a, b, c) in enumerate(TAPS):
                    if c == 2 or (a == 1, b == 1, c == 1) != (te == 1, ke == 1, ce == 1):
                        continue
                    ja = 1 if a < 2 else 0
                    y = dot(cu[b * 3 + c, ja : ja + 4].reshape(64, C), kdt[i * C : (i + 1) * C])
                    total = y if total is None else total + y
                for j in range(4):
                    for kk in range(2):
                        t, k = 2 * j + te, 2 * kk + ke
                        spot = t * 64 + k * W + ce * 8
                        late = (t * 4 + k) * 2 + ce
                        x = pre_ref[spot : spot + 8] + jnp.where(last, fix[late : late + 1], 0.0)
                        s = 1.0 / (1.0 + jnp.exp(-x))
                        at = (j * 2 + kk) * 8
                        g = total[at : at + 8]
                        act32[te * 4 + ke * 2 + ce, at : at + 8] = x * s
                        pre[spot : spot + 8] = g * s * (1.0 + x * (1.0 - s))
    gp[0:2] = jnp.zeros((2, 64, C), BF16)
    gp[2 : T + 2] = pre[...].astype(BF16).reshape(T, 64, C)
    gp[T + 2 : T + 4] = jnp.zeros((2, 64, C), BF16)
    act[...] = act32[...].astype(BF16)


def main_kernel(
    w_ref, xa_ref, xb_ref, edge_ref, gp, act, cu, mine_ref, other_ref, xc, tt
):
    ta, core = lax.axis_index("ta"), lax.rem(lax.axis_index("ha"), 2)

    share = onehot(iota((SHARE, C), 1) == iota((SHARE, C), 0) + ta * SHARE)
    turned = dot_t(share, gp[...].reshape((T + 4) * 64, C))
    left = jnp.concatenate(
        [turned[:, (2 - a) * 64 : (2 - a + T + 2) * 64] for a in range(3)], axis=0
    ).astype(BF16)
    late = edge_ref[...].reshape(6 * 64, 16)
    windows = [xa_ref.at[i] if i < 3 else xb_ref.at[i - 3] for i in range(9)]
    for i in range(6):
        xc[i, 0:2] = jnp.zeros((2, 64, C), BF16)
    for t in range(T):
        built = dot(late, w_ref[t]).astype(BF16)
        for i in range(6):
            base = windows[i // 2 * 3 + i % 2 + 1]
            xc[i, t + 2] = base[t + 2] + built[i * 64 : (i + 1) * 64]
    upper, lower = {}, {}
    for bc in range(9):
        x = windows[bc] if bc % 3 == 0 else xc.at[bc // 3 * 2 + bc % 3 - 1]
        y = dot(left, x[...].reshape((T + 2) * 64, C))
        for a in range(3):
            upper[a * 9 + bc] = y[a * SHARE : (a + 1) * SHARE]
    cots = {}
    for bc in range(9):
        full = dot_t(share, cu[bc].reshape((TA + 1) * 16, C))
        for ja in range(2):
            cots[bc, ja] = full[:, ja * 16 : ja * 16 + 64].astype(BF16)
    for kind in range(8):
        taps = [
            (i, cots[b * 3 + c, 1 if a < 2 else 0])
            for i, (a, b, c) in enumerate(TAPS)
            if (a == 1) * 4 + (b == 1) * 2 + (c == 1) == kind
        ]
        y = dot(jnp.concatenate([x for _, x in taps], axis=0), act[kind])
        for place, (i, _) in enumerate(taps):
            lower[i] = y[place * SHARE : (place + 1) * SHARE]
    for i in range(27):
        both = jnp.concatenate([upper[i], lower[i]], axis=0).astype(BF16)
        tt[i * C : (i + 1) * C] = both.T.astype(F32)
    tt[27 * C :] = jnp.zeros((8, 2 * SHARE), F32)

    def cut(out_ref, parity):
        for x in range(HA // 2):
            for w in range(WA):
                first = ((x * 2 + parity) * WA + w) * PART
                spot = (x * WA + w) * SLOT
                out_ref[spot : spot + SLOT] = tt[first : first + SLOT].astype(BF16)

    for parity in range(2):

        @pl.when(core == parity)
        def _(parity=parity):
            cut(mine_ref, parity)
            cut(other_ref, 1 - parity)


MAIN = (R + 2) * W
WIDE = MAIN + SPILL


def clip_kernel(gp, k1t, own_ref, past_ref, spill_ref, yb, acc):
    later = gp[pl.ds(2 + F * lax.axis_index("ta"), F + 2)]
    for i in range(9):
        b, c = i // 3, i % 3
        pick = jnp.concatenate([clip_pick(b, c, MAIN, W, 0), clip_pick(b, c, SPILL, 2, W)], axis=0)
        for t in range(F + 2):
            yb[i, t] = dot(pick, later[t]).astype(BF16)
    for i, (a, b, c) in enumerate(TAPS):
        x = yb[b * 3 + c, 2 - a : 2 - a + F].reshape(F * WIDE, C)
        y = dot(x, k1t[i * C : (i + 1) * C])
        if i == 0:
            acc[...] = y
        else:
            acc[...] += y
    for f in range(F):
        own_ref[f] = acc[f * WIDE : f * WIDE + R * W]
        past_ref[f] = acc[f * WIDE + R * W : f * WIDE + MAIN].astype(BF16)
        spill_ref[f] = acc[f * WIDE + MAIN : (f + 1) * WIDE].astype(BF16)


def spilled(spill, h):
    place = iota((8, C), 0)
    first, second = spill[2 * h : 2 * h + 1], spill[2 * h + 1 : 2 * h + 2]
    return jnp.where(place == 0, first, jnp.where(place == 1, second, 0.0))


STAGES = 4


def join_kernel(mine_ref, other_ref, after_ref, out_ref, joined, sems):
    rows = PEERS * SLOT // STAGES
    copies = []
    for i in range(STAGES):
        part = pl.ds(i * rows, rows)
        joined[part] = mine_ref[part] + other_ref[part]
        copies.append(pltpu.make_async_copy(joined.at[part], out_ref.at[part], sems.at[i]))
        copies[-1].start()
    for copy in copies:
        copy.wait()


def finish_kernel(
    parts_ref, own_ref, spill_ref, past_ref, corner_ref, clip_out, conv_out, down_out,
    clip_ref, conv_ref, down_ref, sems,
):
    for f in range(F):
        spill, corner = spill_ref[f].astype(F32), corner_ref[f].astype(F32)
        past = past_ref[f].astype(F32)
        for h in range(R):
            at = h * W
            low = own_ref[f, at : at + 8] + spilled(spill, h)
            high = own_ref[f, at + 8 : at + W]
            if h < 2:
                low += past[at : at + 8] + spilled(corner, R + h)
                high += past[at + 8 : at + W]
            clip_ref[f, at : at + W] = jnp.concatenate([low, high], axis=0).astype(BF16)
    leaving = [pltpu.make_async_copy(clip_ref, clip_out, sems.at[0])]
    leaving[0].start()
    total = parts_ref[0].astype(F32)
    for i in range(1, PEERS):
        total += parts_ref[i].astype(F32)
    total = jnp.concatenate([total, jnp.zeros((128 - SLOT, 2 * SHARE), F32)], axis=0).T
    for i, (ref, out) in enumerate(((conv_ref, conv_out), (down_ref, down_out))):
        ref[...] = total[i * SHARE : (i + 1) * SHARE, :PART]
        leaving.append(pltpu.make_async_copy(ref, out, sems.at[i + 1]))
        leaving[-1].start()
    for copy in leaving:
        copy.wait()


def whole():
    return pl.BlockSpec(memory_space=pltpu.VMEM)


def call(kernel, outs, specs, scratch, flops, name, out=None):
    return pl.pallas_call(
        kernel,
        out_shape=outs,
        in_specs=specs,
        out_specs=jax.tree.map(lambda _: out or whole(), outs),
        scratch_shapes=scratch,
        compiler_params=pltpu.CompilerParams(vmem_limit_bytes=VMEM_BYTES),
        cost_estimate=pl.CostEstimate(flops=flops, bytes_accessed=10_000, transcendentals=0),
        name=name,
    )


def shape(dims, dtype=BF16):
    return jax.ShapeDtypeStruct(dims, dtype)


def on_chip(dims, dtype=BF16):
    return pltpu.VMEM(dims, dtype)


def in_hbm(x):
    return pltpu.with_memory_space_constraint(x, pltpu.HBM)


def in_vmem(x):
    return pltpu.with_memory_space_constraint(x, pltpu.VMEM)


def shift(x, axis, by):
    count = lax.axis_size(axis)
    return lax.ppermute(x, axis, [(i, (i + by) % count) for i in range(count)])


def local(clip, conv_weight, down_weight, out_cotangent):
    anywhere = pl.BlockSpec(memory_space=pl.ANY)
    dma = pltpu.SemaphoreType.DMA
    packed = call(
        pack_kernel, shape((BLOCK, C)), [anywhere] * 2, [dma((5,))], 10**5, "pack"
    )(in_hbm(clip.reshape(2 * F, 2 * W, C)), in_hbm(out_cotangent.reshape(-1, C)))
    around = [lax.ppermute(packed, "ta", [(i, i ^ by) for i in range(TA)]) for by in (1, 2, 3)]
    weight = on_chip((27 * C, C))
    k1, k1t, kdt = call(
        load_kernel,
        [weight] * 3,
        [anywhere] * 3,
        [pltpu.VMEM((27 * C, C), BF16), dma((9,)), dma((9,))],
        4 * 10**9,
        "load",
    )(packed, in_hbm(conv_weight), in_hbm(down_weight))
    k1, k1t, kdt = in_vmem(k1), in_vmem(k1t), in_vmem(kdt)
    head = call(
        head_kernel,
        shape((TA, HEAD, C)),
        [whole()] * 4 + [anywhere],
        [],
        10**5,
        "head",
    )(packed, *around, k1t)
    h = shift(head, "ha", -1)
    g, xa, pre = call(
        own_kernel,
        [shape((TA, BLOCK, C)), on_chip((3, T + 2, 64, C)), on_chip((T * 64, C), F32)],
        [whole()] * 4 + [anywhere, whole()],
        [],
        3 * 10**9,
        "own",
    )(packed, *around, head, k1)
    xa, pre = in_vmem(xa), in_vmem(pre)
    w = call(edge_kernel, shape((T, 16, C)), [whole()] * 2, [], 10**7, "edge")(g, h)
    w = shift(w, "wa", -1)
    xb, pre, edge, part = call(
        early_kernel,
        [on_chip((6, T + 2, 64, C)), on_chip((T * 64, C), F32), on_chip((3, 128, 16)), on_chip((4, 64, C), F32)],
        [whole()] * 5,
        [pltpu.VMEM((3, TA + 1, 16, C), BF16)],
        3 * 10**9,
        "early",
    )(g, h, k1, kdt, pre)
    xb, pre, edge, part = in_vmem(xb), in_vmem(pre), in_vmem(edge), in_vmem(part)
    gp, act, cu = call(
        middle_kernel,
        [
            on_chip((T + 4, 64, C)),
            on_chip((8, 64, C)),
            on_chip((9, TA + 1, 16, C)),
        ],
        [whole()] * 7,
        [
            pltpu.VMEM((T * 64, C), F32),
            pltpu.VMEM((8, 64, C), F32),
            pltpu.VMEM((64, C), F32),
        ],
        3 * 10**9,
        "middle",
    )(g, h, w, k1, kdt, pre, part)
    gp, act, cu = in_vmem(gp), in_vmem(act), in_vmem(cu)
    mine, other = call(
        main_kernel,
        [shape((PEERS * SLOT, 2 * SHARE)), shape((PEERS * SLOT, 2 * SHARE))],
        [whole()] * 7,
        [pltpu.VMEM((6, T + 2, 64, C), BF16), pltpu.VMEM((27 * C + 8, 2 * SHARE), F32)],
        5 * 10**9,
        "main",
    )(w, xa, xb, edge, gp, act, cu)
    other = lax.ppermute(other, "ha", [(i, i ^ 1) for i in range(HA)])
    own, past, spill = call(
        clip_kernel,
        [shape((F, R * W, C), F32), shape((F, 2 * W, C)), shape((F, SPILL, C))],
        [whole()] * 2,
        [pltpu.VMEM((9, F + 2, WIDE, C), BF16), pltpu.VMEM((F * WIDE, C), F32)],
        10**9,
        "clip",
    )(gp, k1t)
    pair = call(
        join_kernel,
        shape((PEERS * SLOT, 2 * SHARE)),
        [whole(), whole(), anywhere],
        [pltpu.VMEM((PEERS * SLOT, 2 * SHARE), BF16), dma((STAGES,))],
        10**6,
        "join",
        anywhere,
    )(mine, other, own)
    pairs = [(i * WA + j, (i + 1) % HA * WA + (j + 1) % WA) for i in range(HA) for j in range(WA)]
    corner = lax.ppermute(spill, ("ha", "wa"), pairs)
    spill = shift(spill, "wa", 1)
    past = shift(past, "ha", 1)
    groups = [[i * WA + w for i in range(c, HA, 2) for w in range(WA)] for c in range(2)]
    parts = lax.all_to_all(pair, ("ha", "wa"), 0, 0, axis_index_groups=groups, tiled=True)
    grad_clip, grad_conv, grad_down = call(
        finish_kernel,
        [shape((F, R * W, C)), shape((SHARE, PART), F32), shape((SHARE, PART), F32)],
        [whole()] * 5,
        [
            pltpu.VMEM((F, R * W, C), BF16),
            pltpu.VMEM((SHARE, PART), F32),
            pltpu.VMEM((SHARE, PART), F32),
            dma((3,)),
        ],
        10**6,
        "finish",
        anywhere,
    )(parts.reshape(PEERS, SLOT, 2 * SHARE), own, spill, past, corner)
    grad_clip = grad_clip.reshape(F, R, W, C)
    return (grad_clip, grad_conv.T, grad_down.T)


def solution(mesh):
    return jax.shard_map(
        local,
        mesh=mesh,
        in_specs=(P("ta", "ha", "wa", None), P(), P(), P("ta", "ha", "wa", None)),
        out_specs=(P("ta", "ha", "wa", None), P(("ha", "wa"), "ta"), P(("ha", "wa"), "ta")),
        check_vma=False,
    )
```
